256 devices in a mesh: dp: 8 (over y, z_hi), center: 32 (over z_lo, x, core).
Axes of the slice: x: 4, y: 4, z: 8 (z_hi: 2, z_lo: 4; z = z_hi * 4 + z_lo), core: 2. Of those that a mesh axis runs over, the one named last changes fastest.
Arguments:
- embeddings: bfloat16 [8192, 2048], P('dp', 'center'), may hold values from -6 to 6
- first_weight: bfloat16 [2048, 2048], P(None, 'center'), may hold values from -0.125 to 0.125
- first_bias: float32 [2048], P('center'), may hold values from -3 to 3
- second_weight: bfloat16 [2048, 512], P('center'), may hold values from -0.1875 to 0.1875
- centers: bfloat16 [65536, 512], P('center'), may hold values from -4 to 4
- coefficients: bfloat16 [65536, 100], P('center'), may hold values from -12 to 12
- cotangent: bfloat16 [8192, 100], P('dp'), may hold values from -18 to 18
Outputs:
- predictions: float32 [8192, 100], P(('dp', 'center'))
- grad_first: float32 [2048, 2048], P('dp', 'center')
- grad_bias: float32 [2048], P('center')
- grad_second: float32 [2048, 512], P('center', 'dp')
- grad_centers: float32 [65536, 512], P('center', 'dp')
- grad_coefs: float32 [65536, 100], P('center')
The draws below stay inside these ranges and needn't reach their ends.
All inputs are finite; a program needn't handle non-finite values.
Results may differ from the reference program's by a relative error of at most 0.028.
Values may be sent and summed in bfloat16 or wider, within the bound.
A program may use at most 64 MiB of HBM per device.

```python
import jax
import jax.numpy as jnp
from jax import lax

DIN = 2048
HID = 2048
FEAT = 512
OUT = 100
CDEV = 2048
BATCH = 8192
M = 65536


def block_scale(key, shape, pieces, smallest, largest):
    def one(dim, shards_of):
        heights = jax.random.uniform(jax.random.fold_in(jax.random.fold_in(key, 6), dim), (shards_of,), jnp.float32, smallest / len(pieces), largest / len(pieces))
        return jnp.repeat(jnp.exp(heights), shape[dim] // shards_of).reshape((-1,) + (1,) * (len(shape) - dim - 1))

    gain = one(*pieces[0])
    for cut in pieces[1:]:
        gain = gain * one(*cut)
    return gain


def normal_values(own_key, dims, deviation, reach, split=(), held_as=jnp.bfloat16):
    entries = deviation * jax.random.normal(own_key, dims, jnp.float32)
    if split:
        entries = entries * block_scale(own_key, dims, split, -0.22, 0.18)
    return jnp.clip(entries, -reach, reach).astype(held_as)


def setup_inputs(seed: int = 0) -> dict:
    splits = jax.random.split(jax.random.key(seed), 8)
    embeddings = normal_values(splits[0], (BATCH, DIN), 1.0, 6.0, ((0, 8), (1, 32)))
    first_weight = normal_values(splits[1], (DIN, HID), DIN ** -0.5, 0.125, ((1, 32),))
    first_bias = normal_values(splits[2], (HID,), 0.5, 3.0, ((0, 32),), jnp.float32)
    second_weight = normal_values(splits[3], (HID, FEAT), (HID // 2) ** -0.5, 0.1875, ((0, 32),))
    centers = normal_values(splits[4], (M, FEAT), 0.6, 4.0, ((0, 32),))
    coefficients = normal_values(splits[5], (M, OUT), 2.0, 12.0, ((0, 32),))
    cotangent = normal_values(splits[6], (BATCH, OUT), 3.0, 18.0, ((0, 8),))
    return {"embeddings": embeddings, "first_weight": first_weight, "first_bias": first_bias, "second_weight": second_weight, "centers": centers, "coefficients": coefficients, "cotangent": cotangent}


def reference(embeddings, first_weight, first_bias, second_weight, centers, coefficients, cotangent):
    preact = jnp.dot(embeddings, first_weight, preferred_element_type=jnp.float32) + first_bias
    hidden = jax.nn.gelu(preact).astype(jnp.bfloat16)
    feature_sum = jnp.dot(hidden, second_weight, preferred_element_type=jnp.float32)
    squashed = jnp.tanh(feature_sum)
    features = squashed.astype(jnp.bfloat16)
    feat_wide = features.astype(jnp.float32)
    feat_norms = lax.optimization_barrier(jnp.sum(feat_wide * feat_wide, axis=1))
    factor = 16.0 / FEAT
    block_count = M // CDEV
    center_blocks = centers.reshape(block_count, CDEV, FEAT)
    coef_blocks = coefficients.reshape(block_count, CDEV, OUT)

    def visit(carry, block):
        pred_acc, grad_acc = carry
        center_block, coef_block = block
        center_wide = center_block.astype(jnp.float32)
        center_norms = lax.optimization_barrier(jnp.sum(center_wide * center_wide, axis=1))
        inner_prods = jnp.dot(features, center_block.T, preferred_element_type=jnp.float32)
        sq_dist = feat_norms[:, None] + center_norms[None, :] - 2.0 * inner_prods
        kernel = jnp.exp(-8.0 * sq_dist / FEAT).astype(jnp.bfloat16)
        pred_acc = pred_acc + jnp.dot(kernel, coef_block, preferred_element_type=jnp.float32)
        kernel_grad = jnp.dot(cotangent, coef_block.T, preferred_element_type=jnp.float32)
        weighted = kernel_grad * kernel.astype(jnp.float32)
        weighted_low = weighted.astype(jnp.bfloat16)
        grad_acc = grad_acc - factor * (lax.optimization_barrier(jnp.sum(weighted, axis=1))[:, None] * feat_wide - jnp.dot(weighted_low, center_block, preferred_element_type=jnp.float32))
        center_grad = -factor * (lax.optimization_barrier(jnp.sum(weighted, axis=0))[:, None] * center_wide - jnp.dot(weighted_low.T, features, preferred_element_type=jnp.float32))
        coef_grad = jnp.dot(kernel.T, cotangent, preferred_element_type=jnp.float32)
        return ((pred_acc, grad_acc), (center_grad, coef_grad))
    start_carry = (jnp.zeros((BATCH, OUT), jnp.float32), jnp.zeros((BATCH, FEAT), jnp.float32))
    (predictions, feature_grad), (center_grads, coef_grads) = lax.scan(visit, start_carry, (center_blocks, coef_blocks))
    grad_centers = center_grads.reshape(M, FEAT)
    grad_coefs = coef_grads.reshape(M, OUT)
    phi_grad = (feature_grad * (1.0 - squashed * squashed)).astype(jnp.bfloat16)
    grad_second = jnp.dot(hidden.T, phi_grad, preferred_element_type=jnp.float32)
    hidden_grad = jnp.dot(phi_grad, second_weight.T, preferred_element_type=jnp.float32)
    unused, pullback = jax.vjp(jax.nn.gelu, preact)
    preact_grad = pullback(hidden_grad)[0]
    grad_bias = lax.optimization_barrier(jnp.sum(preact_grad, axis=0))
    preact_low = preact_grad.astype(jnp.bfloat16)
    grad_first = jnp.dot(embeddings.T, preact_low, preferred_element_type=jnp.float32)
    return (predictions, grad_first, grad_bias, grad_second, grad_centers, grad_coefs)
```

```python
import functools
import math

import jax
import jax.numpy as jnp
from jax import lax
from jax.experimental import pallas as pl
from jax.experimental.pallas import tpu as pltpu
from jax.sharding import PartitionSpec as P

MESH = pl.DeviceIdType.MESH
F32 = jnp.float32
BF16 = jnp.bfloat16
ORDER = (0, 1, 3, 2)
GELU_C = math.sqrt(2.0 / math.pi)
LOG2E = math.log2(math.e)
SEMS = 96


def dot(a, b):
    return jnp.dot(a, b, preferred_element_type=F32)


def kernel(emb, w1, b1, w2, ctr, coef, cot,
           o_pred, o_first, o_second, o_bias, o_cg, o_coef,
           emb_sib, emb_pair, w_sib, w_pair, b_mine, b_sib, b_pair, wg, sg, bg, g, gt,
           pre, hid, gd, part, part_in, zs, zown, zr, sq, f, ft, ct, qp, qt, cn, cotp, cott,
           fg, pr, rs, cg, cf, cs, rp, prv, xown, xs_out, xr, z2, z2own, z2r, ph,
           cgs, cgr, cgh, cghr, cfs, cfr, cfh, cfhr, tt, tr, u, v, hs, hb, tot,
           ssem, rsem):
    dp = lax.axis_index("dp")
    c = lax.axis_index("center")
    y, h = dp // 2, dp % 2
    zl, x, k = c // 8, (c // 2) % 4, c % 2
    feat = 512
    factor = 16.0 / feat
    scale = 8.0 / feat * LOG2E

    def dev(xx=None, yy=None, hh=None, zz=None, kk=None):
        xx = x if xx is None else xx
        yy = y if yy is None else yy
        hh = h if hh is None else hh
        zz = zl if zz is None else zz
        kk = k if kk is None else kk
        return {"dp": yy * 2 + hh, "center": zz * 8 + xx * 2 + kk}

    def plus(a, d):
        return lax.rem(a + d, 4)

    def minus(a, d):
        return lax.rem(a + 4 - d, 4)

    ids = {"s": 0, "r": 0}
    sent = []

    def new(kind, n=1):
        first = ids[kind]
        ids[kind] += n
        assert ids[kind] <= SEMS
        return first

    def remote(src, dst, target, sid, rid):
        return pltpu.make_async_remote_copy(
            src_ref=src, dst_ref=dst, send_sem=ssem.at[sid], recv_sem=rsem.at[rid],
            device_id=target, device_id_type=MESH)

    def send(src, dst, target, rid=None):
        rid = new("r") if rid is None else rid
        cp = remote(src, dst, target, new("s"), rid)
        cp.start()
        sent.append(cp)
        return cp

    def to_home(src, dst_at, rid_at):
        rid = rid_at
        for d in (1, 3, 2):
            send(src, dst_at, dev(xx=plus(x, d), kk=x // 2), rid)
        sid = new("s")

        @pl.when(k == x // 2)
        def _():
            pltpu.make_async_copy(src, dst_at, rsem.at[rid]).start()

        @pl.when(k != x // 2)
        def _():
            remote(src, dst_at, dev(kk=1 - k), sid, rid).start()
        homes.append((src, dst_at, sid))

    homes = []

    barrier = pltpu.get_barrier_semaphore()
    peers = [dev(kk=1 - k), dev(hh=1 - h)]
    for d in (1, 2, 3):
        peers += [dev(xx=plus(x, d)), dev(xx=plus(x, d), kk=1 - k), dev(zz=plus(zl, d)), dev(yy=plus(y, d))]
    for peer in peers:
        pl.semaphore_signal(barrier, inc=1, device_id=peer, device_id_type=MESH)
    b_mine[...] = jnp.broadcast_to(b1[...], b_mine.shape)
    pl.semaphore_wait(barrier, len(peers))
    sib = dev(kk=1 - k)

    c_emb = send(emb.at[:, :, 1 - k], emb_sib, sib)
    c_w = send(w1.at[1 - k], w_sib, sib)
    c_b = send(b_mine, b_sib, sib)

    r_sg = new("r", 4)
    to_home(w2, sg.at[x % 2, k], r_sg + 2 * (x % 2) + k)

    def paired(mine, other):
        low = jnp.where(k == 0, mine, other)
        high = jnp.where(k == 0, other, mine)
        return jnp.concatenate([low, high], axis=-1)

    c_emb.wait_recv()
    for xx in range(4):
        emb_pair[xx] = paired(emb[:, xx, k].reshape(128, 64), emb_sib[:, xx].reshape(128, 64))
    c_x = {}
    for d in (1, 3, 2):
        c_x[d] = send(emb_pair.at[plus(x, d)], g.at[zl, x, k], dev(xx=plus(x, d)))
    g[zl, x, k] = emb_pair[x]

    c_w.wait_recv()
    w_pair[...] = paired(w1[k], w_sib[...]).reshape(2, 512, 128)
    r_w = new("r", 4)
    to_home(w_pair, wg.at[x % 2, pl.ds(2 * k, 2)], r_w + 2 * (x % 2) + k)
    c_b.wait_recv()
    b_pair[...] = paired(b_mine[:, :64], b_sib[:, :64])
    r_b = new("r", 4)
    to_home(b_pair, bg.at[x % 2, k], r_b + 2 * (x % 2) + k)

    c_z = {}
    for d in ORDER:
        xx = minus(x, d)
        if d:
            c_x[d].wait_recv()
        piece = g.at[zl, xx, k]
        for e in (1, 3, 2):
            c_z[d, e] = send(piece, piece, dev(zz=plus(zl, e)))
    c_gs = {0: send(g.at[zl, :, k], g.at[zl, :, k], sib)}

    qp[...] = jnp.zeros_like(qp)
    cotp[...] = jnp.zeros_like(cotp)
    for xx in range(4):
        for kk in range(2):
            for zz in range(4):
                cotp[xx, pl.ds((kk * 4 + zz) * 32, 32), :100] = cot[zz, xx, kk]

    def prepare(t, carry):
        qp[t, :, :100] = coef[t]
        qt[t] = qp[t].T
        turned = ctr[t].T
        ct[t] = turned
        wide = turned.astype(F32)
        cn[t] = jnp.broadcast_to(jnp.sum(wide * wide, axis=0, keepdims=True) * scale, (8, 512))
        cott[t] = cotp[t].T
        cg[t] = jnp.zeros((512, 512), F32)
        cf[t] = jnp.zeros((128, 512), F32)
        cs[t] = jnp.zeros((8, 512), F32)
        return carry

    lax.fori_loop(0, 4, prepare, 0)

    def wait_home(ref, first):
        for i in range(2):
            for j in range(2):
                pltpu.make_async_copy(ref.at[i, pl.ds(2 * j, 2)] if ref is wg else ref.at[i, j],
                                      ref.at[i, pl.ds(2 * j, 2)] if ref is wg else ref.at[i, j],
                                      rsem.at[first + 2 * i + j]).wait()

    wait_home(sg, r_sg)
    wait_home(wg, r_w)
    wait_home(bg, r_b)

    acc = jnp.zeros((256, 256), F32)
    for e in ORDER:
        src = minus(zl, e)
        if e:
            for d in ORDER:
                c_z[d, e].wait_recv()
            c_gs[e] = send(g.at[src, :, k], g.at[src, :, k], sib)
        c_gs[e].wait_recv()
        lhs = jnp.concatenate([g[src, xx].reshape(256, 128) for xx in range(4)], axis=1)
        rhs = jnp.concatenate([wg[0, src], wg[1, src]], axis=1)
        acc = acc + dot(lhs, rhs)
    bias = jnp.concatenate([bg[0, 0], bg[1, 0]], axis=1)[0:1]
    pre[...] = acc + bias
    u0 = pre[...]
    t0 = jnp.tanh(GELU_C * (u0 + 0.044715 * (u0 * u0 * u0)))
    hid[...] = (u0 * (0.5 * (1.0 + t0))).astype(BF16)
    second = sg[...].reshape(256, 512)
    part[...] = dot(hid[...], second).reshape(2, 128, 512)
    c_p = send(part.at[1 - k], part_in, sib)
    gd[...] = 0.5 * (1.0 + t0) + 0.5 * u0 * (1.0 - t0 * t0) * (GELU_C * (1.0 + 3.0 * 0.044715 * (u0 * u0)))
    c_p.wait_recv()
    summed = (part[k] + part_in[...]).reshape(4, 32, 512)
    zown[...] = summed
    zs[...] = summed.astype(BF16)
    c_f = {}
    for e in (1, 3, 2):
        c_f[e] = send(zs.at[plus(zl, e)], zr.at[e - 1], dev(zz=plus(zl, e)))
    for zz in range(4):
        for xx in range(4):
            gt[zz * 2 + xx // 2, pl.ds((xx % 2) * 128, 128)] = g[zz, xx].reshape(256, 128).T
    total = zown[zl]
    for e in (1, 3, 2):
        c_f[e].wait_recv()
        total = total + zr[e - 1].astype(F32)
    squashed = jnp.tanh(total)
    sq[...] = squashed
    f[x, k, zl] = squashed.astype(BF16)

    c_fz = [send(f.at[x, k, zl], f.at[x, k, zl], dev(zz=plus(zl, e))) for e in (1, 3, 2)]
    for cp in c_fz:
        cp.wait_recv()
    c_fs = {0: send(f.at[x, k], f.at[x, k], sib)}
    c_fx = {d: send(f.at[x, k], f.at[x, k], dev(xx=plus(x, d))) for d in (1, 3, 2)}

    c_pair = {}
    c_xr = {}

    def finish_pair(i):
        c_pair[i].wait_recv()
        both = rp[i, k].astype(F32) + prv[i].astype(F32)
        if i == 0:
            xown[...] = both
        else:
            xs_out[i - 1] = both.astype(BF16)
            c_xr[i] = send(xs_out.at[i - 1], xr.at[i - 1], dev(xx=minus(x, ORDER[i])))

    for i, d in enumerate(ORDER):
        xx = minus(x, d)
        c_fs[d].wait_recv()
        fx = f[xx].reshape(256, 512)
        wide = fx.astype(F32)
        fn = jnp.sum(wide * wide, axis=1, keepdims=True) * scale
        ft[...] = fx.T
        fg[...] = jnp.zeros_like(fg)
        pr[...] = jnp.zeros_like(pr)
        rs[...] = jnp.zeros_like(rs)

        def tile(t, carry):
            fx = f[xx].reshape(256, 512)
            inner = dot(fx, ct[t])
            low = jnp.exp2((2.0 * scale) * inner - (fn + cn[t, 0:1])).astype(BF16)
            weighted = dot(cotp[xx], qt[t]) * low.astype(F32)
            wlow = weighted.astype(BF16)
            rs[...] += (weighted[:, 0:128] + weighted[:, 128:256]) + (weighted[:, 256:384] + weighted[:, 384:512])
            cs[t] += jnp.sum(weighted.reshape(32, 8, 512), axis=0)
            pr[...] += dot(low, qp[t])
            fg[...] += dot(wlow, ctr[t])
            cg[t] += dot(ft[...], wlow)
            cf[t] += dot(cott[xx], low)
            return carry

        lax.fori_loop(0, 2, tile, 0)
        if i < 3:
            nxt = ORDER[i + 1]
            c_fx[nxt].wait_recv()
            c_fs[nxt] = send(f.at[minus(x, nxt), k], f.at[minus(x, nxt), k], sib)
        if i > 0:
            finish_pair(i - 1)
        lax.fori_loop(2, 4, tile, 0)
        fx = f[xx].reshape(256, 512)
        rows = jnp.sum(rs[...], axis=1, keepdims=True)
        fgrad = -factor * (rows * fx.astype(F32) - fg[...])
        rp[i, :, :, :512] = fgrad.astype(BF16).reshape(2, 128, 512)
        rp[i, :, :, 512:] = pr[...].astype(BF16).reshape(2, 128, 128)
        c_pair[i] = send(rp.at[i, 1 - k], prv.at[i], sib)

    def center_out(t, carry):
        column = jnp.sum(cs[t], axis=0, keepdims=True)
        grad = -factor * (column * ct[t].astype(F32) - cg[t])
        cgs[:, t] = grad.astype(BF16).reshape(4, 128, 512)
        cfs[t] = cf[t, 0:112].astype(BF16)
        return carry

    lax.fori_loop(0, 4, center_out, 0)
    finish_pair(3)
    c_cg = {e: send(cgs.at[plus(y, e)], cgr.at[e - 1], dev(yy=plus(y, e))) for e in (1, 3, 2)}
    r_cf = new("r", 4)
    for e in (1, 3, 2):
        send(cfs.at[plus(y, e)], cfr.at[y], dev(yy=plus(y, e)), r_cf + y)
    cfr[y] = cfs[y]

    total = xown[...]
    for i in (1, 2, 3):
        c_xr[i].wait_recv()
        total = total + xr[i - 1].astype(F32)
    total = total.reshape(4, 32, 640)
    z2own[...] = total
    z2[...] = total.astype(BF16)
    c_z2 = {e: send(z2.at[plus(zl, e)], z2r.at[e - 1], dev(zz=plus(zl, e))) for e in (1, 3, 2)}
    total = z2own[zl]
    for e in (1, 3, 2):
        c_z2[e].wait_recv()
        total = total + z2r[e - 1].astype(F32)
    o_pred[...] = total[:, 512:612]
    phi = (total[:, :512] * (1.0 - sq[...] * sq[...])).astype(BF16)
    ph[k, zl] = phi
    c_ph = [send(ph.at[k, zl], ph.at[k, zl], dev(zz=plus(zl, e))) for e in (1, 3, 2)]
    for cp in c_ph:
        cp.wait_recv()
    c_phs = send(ph.at[k], ph.at[k], sib)
    c_phs.wait_recv()

    phi_all = ph[...].reshape(256, 512)
    hgrad = lax.dot_general(phi_all, sg[...].reshape(256, 512), (((1,), (1,)), ((), ())), preferred_element_type=F32)
    pgrad = hgrad * gd[...]
    bias_grad = jnp.sum(pgrad, axis=0, keepdims=True)
    plow = pgrad.astype(BF16)
    phit = phi_all.T
    bias_rows = jnp.broadcast_to(bias_grad, (16, 256)).astype(BF16)
    second_grad = dot(phit, hid[...]).astype(BF16)
    for yy in range(4):
        for hh in range(2):
            q = 2 * yy + hh
            tt[yy, hh, 0:256] = dot(gt[q], plow).astype(BF16)
            tt[yy, hh, 256:320] = second_grad[64 * q:64 * q + 64]
            tt[yy, hh, 320:336] = bias_rows
    r_t = new("r", 4)
    for e in (2, 1, 3):
        send(tt.at[plus(y, e)], tr.at[y], dev(yy=plus(y, e)), r_t + y)
    tr[y] = tt[y]

    for e in (1, 3, 2):
        c_cg[e].wait_recv()

    def center_sum(t, carry):
        s = cgs[y, t].astype(F32)
        for e in (1, 3, 2):
            s = s + cgr[e - 1, t].astype(F32)
        s = s.reshape(2, 64, 512)
        cgh[t] = s.astype(BF16)
        o_cg[t] = jnp.where(h == 0, s[0], s[1])
        return carry

    lax.fori_loop(0, 4, center_sum, 0)
    c_ch = send(cgh.at[:, 1 - h], cghr, dev(hh=1 - h))

    def wait_slots(ref, first, own):
        for j in range(4):
            @pl.when(own != j)
            def _():
                pltpu.make_async_copy(ref.at[j], ref.at[j], rsem.at[first + j]).wait()

    wait_slots(cfr, r_cf, y)
    s = (cfr[0].astype(F32) + cfr[1].astype(F32)) + (cfr[2].astype(F32) + cfr[3].astype(F32))
    cfh[...] = s.astype(BF16)
    c_cfh = send(cfh, cfhr, dev(hh=1 - h))

    wait_slots(tr, r_t, y)
    for hh in range(2):
        s = (tr[0, hh].astype(F32) + tr[1, hh].astype(F32)) + (tr[2, hh].astype(F32) + tr[3, hh].astype(F32))
        low = s.astype(BF16)
        u[0, hh] = low[:, :128]
        u[1, hh] = low[:, 128:]
    r_v = new("r", 4)
    x_sends = []
    for j in range(2):
        for hh in range(2):
            sid = new("s")
            mine = jnp.logical_and(x == 2 * k + j, k == hh)
            src, dst, rid = u.at[j, hh], v.at[x], r_v + x
            x_sends.append((src, dst, sid, mine))

            @pl.when(mine)
            def _():
                pltpu.make_async_copy(src, dst, rsem.at[rid]).start()

            @pl.when(jnp.logical_not(mine))
            def _():
                remote(src, dst, dev(xx=2 * k + j, kk=hh), sid, rid).start()

    c_cfh.wait_recv()
    o_coef[y] = (cfh[...].astype(F32) + cfhr[...].astype(F32)).astype(BF16)
    r_o = new("r", 4)
    for e in (1, 3, 2):
        send(o_coef.at[y], o_coef.at[y], dev(yy=plus(y, e)), r_o + y)

    for j in range(4):
        pltpu.make_async_copy(v.at[j], v.at[j], rsem.at[r_v + j]).wait()
    s = (v[0].astype(F32) + v[1].astype(F32)) + (v[2].astype(F32) + v[3].astype(F32))
    hs[...] = s.astype(BF16)
    s_across, r_across, s_last, r_last = new("s"), new("r"), new("s"), new("r")

    @pl.when(k != h)
    def _():
        remote(hs, hb, dev(hh=1 - h, kk=k), s_across, r_across).start()

    c_ch.wait_recv()
    o_cg[...] += cghr[...].astype(F32)

    @pl.when(k == h)
    def _():
        pltpu.make_async_copy(hb, hb, rsem.at[r_across]).wait()
        tot[...] = hs[...].astype(F32) + hb[...].astype(F32)
        remote(tot, tot, sib, s_last, r_last).start()

    @pl.when(k != h)
    def _():
        pltpu.make_async_copy(tot, tot, rsem.at[r_last]).wait()

    whole = tot[...]
    half = jnp.where(k == 0, whole[:, :64], whole[:, 64:])
    o_first[...] = half[0:256]
    o_second[...] = half[256:320]
    o_bias[...] = half[320:328]
    wait_slots(o_coef, r_o, y)

    for cp in sent:
        cp.wait_send()
    for src, dst, sid in homes:
        @pl.when(k != x // 2)
        def _():
            pltpu.make_async_copy(src, src, ssem.at[sid]).wait()
    for src, dst, sid, mine in x_sends:
        @pl.when(jnp.logical_not(mine))
        def _():
            pltpu.make_async_copy(src, src, ssem.at[sid]).wait()

    @pl.when(k != h)
    def _():
        pltpu.make_async_copy(hs, hs, ssem.at[s_across]).wait()

    @pl.when(k == h)
    def _():
        pltpu.make_async_copy(tot, tot, ssem.at[s_last]).wait()


SCRATCH = (
    ("emb_sib", (4, 4, 32, 64), BF16), ("emb_pair", (4, 128, 128), BF16), ("w_sib", (1024, 64), BF16),
    ("w_pair", (2, 512, 128), BF16), ("b_mine", (8, 128), F32), ("b_sib", (8, 128), F32), ("b_pair", (8, 128), F32),
    ("wg", (2, 4, 512, 128), BF16), ("sg", (2, 2, 64, 512), BF16), ("bg", (2, 2, 8, 128), F32),
    ("g", (4, 4, 2, 128, 128), BF16), ("gt", (8, 256, 256), BF16),
    ("pre", (256, 256), F32), ("hid", (256, 256), BF16), ("gd", (256, 256), F32),
    ("part", (2, 128, 512), F32), ("part_in", (128, 512), F32),
    ("zs", (4, 32, 512), BF16), ("zown", (4, 32, 512), F32), ("zr", (3, 32, 512), BF16), ("sq", (32, 512), F32),
    ("f", (4, 2, 4, 32, 512), BF16), ("ft", (512, 256), BF16), ("ct", (4, 512, 512), BF16),
    ("qp", (4, 512, 128), BF16), ("qt", (4, 128, 512), BF16), ("cn", (4, 8, 512), F32),
    ("cotp", (4, 256, 128), BF16), ("cott", (4, 128, 256), BF16),
    ("fg", (256, 512), F32), ("pr", (256, 128), F32), ("rs", (256, 128), F32),
    ("cg", (4, 512, 512), F32), ("cf", (4, 128, 512), F32), ("cs", (4, 8, 512), F32),
    ("rp", (4, 2, 128, 640), BF16), ("prv", (4, 128, 640), BF16), ("xown", (128, 640), F32),
    ("xs_out", (3, 128, 640), BF16), ("xr", (3, 128, 640), BF16),
    ("z2", (4, 32, 640), BF16), ("z2own", (4, 32, 640), F32), ("z2r", (3, 32, 640), BF16), ("ph", (2, 4, 32, 512), BF16),
    ("cgs", (4, 4, 128, 512), BF16), ("cgr", (3, 4, 128, 512), BF16), ("cgh", (4, 2, 64, 512), BF16), ("cghr", (4, 64, 512), BF16),
    ("cfs", (4, 112, 512), BF16), ("cfr", (4, 112, 512), BF16), ("cfh", (112, 512), BF16), ("cfhr", (112, 512), BF16),
    ("tt", (4, 2, 336, 256), BF16), ("tr", (4, 2, 336, 256), BF16), ("u", (2, 2, 336, 128), BF16),
    ("v", (4, 336, 128), BF16), ("hs", (336, 128), BF16), ("hb", (336, 128), BF16), ("tot", (336, 128), F32),
)


def body(embeddings, first_weight, first_bias, second_weight, centers, coefficients, cotangent):
    args = (
        embeddings.reshape(4, 4, 2, 32, 64),
        first_weight.reshape(2, 1024, 64),
        jnp.pad(first_bias.reshape(1, 64), ((0, 0), (0, 64))),
        second_weight,
        centers.reshape(4, 512, 512),
        coefficients.reshape(4, 512, 100),
        cotangent.reshape(4, 4, 2, 32, 100),
    )
    vmem = pl.BlockSpec(memory_space=pltpu.VMEM)
    outs = (
        jax.ShapeDtypeStruct((32, 100), F32),
        jax.ShapeDtypeStruct((256, 64), F32),
        jax.ShapeDtypeStruct((64, 64), F32),
        jax.ShapeDtypeStruct((8, 64), F32),
        jax.ShapeDtypeStruct((4, 64, 512), F32),
        jax.ShapeDtypeStruct((4, 112, 512), BF16),
    )
    predictions, grad_first, grad_second, grad_bias, grad_centers, grad_coefs = pl.pallas_call(
        kernel,
        out_shape=outs,
        in_specs=[vmem] * len(args),
        out_specs=[vmem] * len(outs),
        scratch_shapes=[pltpu.VMEM(shape, dtype) for name, shape, dtype in SCRATCH]
        + [pltpu.SemaphoreType.DMA((SEMS,)), pltpu.SemaphoreType.DMA((SEMS,))],
        compiler_params=pltpu.CompilerParams(collective_id=0, has_side_effects=True, vmem_limit_bytes=60 << 20),
        name="layer",
    )(*args)
    return (
        predictions,
        grad_first,
        grad_bias[0],
        grad_second.T,
        grad_centers.transpose(0, 2, 1).reshape(2048, 64),
        grad_coefs.transpose(0, 2, 1)[:, :, :100].reshape(2048, 100).astype(F32),
    )


def solution(mesh):
    placed = (
        P("dp", "center"),
        P(None, "center"),
        P("center"),
        P("center", None),
        P("center", None),
        P("center", None),
        P("dp", None),
    )
    return jax.shard_map(
        body,
        mesh=mesh,
        in_specs=placed,
        out_specs=(
            P(("dp", "center"), None),
            P("dp", "center"),
            P("center"),
            P("center", "dp"),
            P("center", "dp"),
            P("center", None),
        ),
        check_vma=False,
    )
```

```python
import functools
import math

import jax
import jax.numpy as jnp
from jax import lax
from jax.experimental import pallas as pl
from jax.experimental.pallas import tpu as pltpu
from jax.sharding import PartitionSpec as P

MESH = pl.DeviceIdType.MESH
F32 = jnp.float32
BF16 = jnp.bfloat16
ORDER = (0, 1, 3, 2)
GELU_C = math.sqrt(2.0 / math.pi)
LOG2E = math.log2(math.e)
SEMS = 160


def dot(a, b):
    return jnp.dot(a, b, preferred_element_type=F32)


def kernel(embt_hbm, w1t_hbm, b1, w2, ctr_hbm, coeft_hbm, cott_hbm,
           o_pred, o_first, o_second, o_bias, o_cg, o_coef,
           embt, w1t, ctr, coeft, cott_in, emb_sib, emb_all, w_sib, w_pair, b_mine, b_sib, b_pair, wg, sg, bg, g, gt,
           hid, gd, part, part_in, zs, zown, zr, sq, f, ft, ct,
           qp, qt, cn, cot_pad, cot_all, cotp, cott, kg, kb, wb,
           rs, cs, rp, prv, xown, xs_out, xr, z2, z2own, z2r, ph,
           cgs, cgr, cgh, cghr, cfs, cfr, cfh, cfhr, tt, tr, u, v, tb, vb, ub, yb, mix, hs, ha, hb,
           ssem, rsem):
    dp = lax.axis_index("dp")
    c = lax.axis_index("center")
    y, h = dp // 2, dp % 2
    zl, x, k = c // 8, (c // 2) % 4, c % 2
    feat = 512
    factor = 16.0 / feat
    scale = 8.0 / feat * LOG2E

    def dev(xx=None, yy=None, hh=None, zz=None, kk=None):
        xx = x if xx is None else xx
        yy = y if yy is None else yy
        hh = h if hh is None else hh
        zz = zl if zz is None else zz
        kk = k if kk is None else kk
        return {"dp": yy * 2 + hh, "center": zz * 8 + xx * 2 + kk}

    def plus(a, d):
        return lax.rem(a + d, 4)

    def minus(a, d):
        return lax.rem(a + 4 - d, 4)

    ids = {"s": 0, "r": 0}
    sent = []

    def new(kind, n=1):
        first = ids[kind]
        ids[kind] += n
        assert ids[kind] <= SEMS
        return first

    def remote(src, dst, target, sid, rid):
        return pltpu.make_async_remote_copy(
            src_ref=src, dst_ref=dst, send_sem=ssem.at[sid], recv_sem=rsem.at[rid],
            device_id=target, device_id_type=MESH)

    def send(src, dst, target, rid=None):
        rid = new("r") if rid is None else rid
        cp = remote(src, dst, target, new("s"), rid)
        cp.start()
        sent.append(cp)
        return cp

    def to_home(src, dst_at, rid_at):
        rid = rid_at
        for d in (1, 3, 2):
            send(src, dst_at, dev(xx=plus(x, d), kk=x // 2), rid)
        sid = new("s")

        @pl.when(k == x // 2)
        def _():
            pltpu.make_async_copy(src, dst_at, rsem.at[rid]).start()

        @pl.when(k != x // 2)
        def _():
            remote(src, dst_at, dev(kk=1 - k), sid, rid).start()
        homes.append((src, dst_at, sid))

    homes = []

    barrier = pltpu.get_barrier_semaphore()
    peers = [dev(kk=1 - k), dev(hh=1 - h), dev(hh=1 - h, kk=1 - k)]
    for d in (1, 2, 3):
        peers += [dev(xx=plus(x, d)), dev(xx=plus(x, d), kk=1 - k), dev(zz=plus(zl, d)), dev(yy=plus(y, d))]
    for peer in peers:
        pl.semaphore_signal(barrier, inc=1, device_id=peer, device_id_type=MESH)
    loads = []
    own_half = pl.ds(pl.multiple_of(k * 1024, 1024), 1024)
    for src, dst in ((embt_hbm, embt), (w1t_hbm.at[:, own_half], w1t), (cott_hbm, cott_in), (coeft_hbm, coeft), (ctr_hbm, ctr)):
        loads.append(pltpu.make_async_copy(src, dst, rsem.at[new("r")]))
        loads[-1].start()
    wide_bias = jnp.broadcast_to(b1[...], (8, 64))
    b_mine[...] = jnp.concatenate([wide_bias, wide_bias], axis=1)
    pl.semaphore_wait(barrier, len(peers))
    sib = dev(kk=1 - k)

    c_emb = send(embt_hbm, emb_sib, sib)
    c_w = send(w1t_hbm.at[:, pl.ds(pl.multiple_of((1 - k) * 1024, 1024), 1024)], w_sib, sib)
    c_b = send(b_mine, b_sib, sib)

    def paired(mine, other):
        low = jnp.where(k == 0, mine, other)
        high = jnp.where(k == 0, other, mine)
        return jnp.concatenate([low, high], axis=0)

    loads[0].wait()
    c_emb.wait_recv()
    emb_all[...] = paired(embt[...], emb_sib[...]).T.reshape(4, 4, 2, 32, 128)
    c_x = {}
    for d in (1, 3, 2):
        c_x[d] = send(emb_all.at[:, plus(x, d), k], g.at[zl, x, k], dev(xx=plus(x, d)))
    g[zl, x, k] = emb_all[:, x, k]

    loads[1].wait()
    c_w.wait_recv()
    w_pair[...] = paired(w1t[...], w_sib[...]).T.reshape(2, 512, 128)
    r_w = new("r", 4)
    to_home(w_pair, wg.at[x % 2, pl.ds(2 * k, 2)], r_w + 2 * (x % 2) + k)
    c_b.wait_recv()
    lane = lax.broadcasted_iota(jnp.int32, (8, 128), 1)
    b_pair[...] = jnp.where((lane < 64) == (k == 0), b_mine[...], b_sib[...])
    r_b = new("r", 4)
    to_home(b_pair, bg.at[x % 2, k], r_b + 2 * (x % 2) + k)

    r_sg = new("r", 4)
    to_home(w2, sg.at[x % 2, k], r_sg + 2 * (x % 2) + k)

    c_z = {}
    for d in ORDER:
        xx = minus(x, d)
        if d:
            c_x[d].wait_recv()
        piece = g.at[zl, xx, k]
        for e in (1, 3, 2):
            c_z[d, e] = send(piece, piece, dev(zz=plus(zl, e)))
    c_gs = {0: send(g.at[zl, :, k], g.at[zl, :, k], sib)}

    for load in loads[2:]:
        load.wait()
    cot_pad[...] = jnp.zeros_like(cot_pad)
    cot_pad[0:100] = cott_in[...]
    cot_all[...] = cot_pad[...].T.reshape(4, 4, 2, 32, 128)
    for xx in range(4):
        for kk in range(2):
            cotp[xx, kk * 128:kk * 128 + 128] = cot_all[:, xx, kk].reshape(128, 128)
        cott[xx] = cotp[xx].T
    qt[...] = jnp.zeros_like(qt)
    for t in range(4):
        qt[t, 0:100] = coeft[:, t * 512:t * 512 + 512]

    def prepare(t, carry):
        rows = pl.ds(pl.multiple_of(t * 512, 512), 512)
        qp[rows] = qt[t].T
        turned = ctr[rows].T
        ct[t] = turned
        wide = turned.astype(F32)
        cn[t] = jnp.broadcast_to(jnp.sum(wide * wide, axis=0, keepdims=True) * scale, (8, 512))
        cs[t] = jnp.zeros((8, 512), F32)
        rs[t] = jnp.zeros((256, 128), F32)
        for xx in range(4):
            kg[xx, t] = dot(cotp[xx], qt[t])
        return carry

    lax.fori_loop(0, 4, prepare, 0)

    def wait_home(ref, first):
        for i in range(2):
            for j in range(2):
                pltpu.make_async_copy(ref.at[i, pl.ds(2 * j, 2)] if ref is wg else ref.at[i, j],
                                      ref.at[i, pl.ds(2 * j, 2)] if ref is wg else ref.at[i, j],
                                      rsem.at[first + 2 * i + j]).wait()

    wait_home(wg, r_w)

    acc = jnp.zeros((256, 256), F32)
    for n, e in enumerate(ORDER):
        src = minus(zl, e)
        if n < 3:
            nxt = ORDER[n + 1]
            for d in ORDER:
                c_z[d, nxt].wait_recv()
            c_gs[nxt] = send(g.at[minus(zl, nxt), :, k], g.at[minus(zl, nxt), :, k], sib)
        c_gs[e].wait_recv()
        lhs = jnp.concatenate([g[src, xx].reshape(256, 128) for xx in range(4)], axis=1)
        rhs = jnp.concatenate([wg[0, src], wg[1, src]], axis=1)
        acc = acc + dot(lhs, rhs)
    wait_home(bg, r_b)
    wait_home(sg, r_sg)
    bias = jnp.concatenate([bg[0, 0], bg[1, 0]], axis=1)[0:1]
    u0 = acc + bias
    t0 = jnp.tanh(GELU_C * (u0 + 0.044715 * (u0 * u0 * u0)))
    hid[...] = (u0 * (0.5 * (1.0 + t0))).astype(BF16)
    second = sg[...].reshape(256, 512)
    part[...] = dot(hid[...], second).reshape(2, 128, 512)
    c_p = send(part.at[1 - k], part_in, sib)
    gd[...] = 0.5 * (1.0 + t0) + 0.5 * u0 * (1.0 - t0 * t0) * (GELU_C * (1.0 + 3.0 * 0.044715 * (u0 * u0)))
    c_p.wait_recv()
    summed = (part[k] + part_in[...]).reshape(4, 32, 512)
    zown[...] = summed
    zs[...] = summed.astype(BF16)
    c_f = {}
    for e in (1, 3, 2):
        c_f[e] = send(zs.at[plus(zl, e)], zr.at[e - 1], dev(zz=plus(zl, e)))
    for zz in range(4):
        for xx in range(4):
            gt[zz * 2 + xx // 2, pl.ds((xx % 2) * 128, 128)] = g[zz, xx].reshape(256, 128).T
    total = zown[zl]
    for e in (1, 3, 2):
        c_f[e].wait_recv()
        total = total + zr[e - 1].astype(F32)
    squashed = jnp.tanh(total)
    sq[...] = squashed
    f[x, k, zl] = squashed.astype(BF16)

    own_piece = f.at[x, k, zl]
    c_fz = {e: send(own_piece, own_piece, dev(zz=plus(zl, e))) for e in (1, 3, 2)}
    c_fx = {}
    c_fp = {}
    for e in ORDER:
        if e:
            c_fz[e].wait_recv()
        piece = f.at[x, k, minus(zl, e)]
        c_fp[e] = send(piece, piece, sib)
        for d in (1, 3, 2):
            c_fx[d, e] = send(piece, piece, dev(xx=plus(x, d)))
    c_fs = {}

    def forward(d):
        for e in ORDER:
            c_fx[d, e].wait_recv()
        block = f.at[minus(x, d), k]
        c_fs[d] = send(block, block, sib)

    c_pair = {}
    c_xr = {}

    def finish_pair(i):
        c_pair[i].wait_recv()
        both = rp[i, k].astype(F32) + prv[i].astype(F32)
        if i == 0:
            xown[...] = both
        else:
            xs_out[i - 1] = both.astype(BF16)
            c_xr[i] = send(xs_out.at[i - 1], xr.at[i - 1], dev(xx=minus(x, ORDER[i])))

    def weigh(i, first, last):
        xx = minus(x, ORDER[i])
        here = slice(256 * i, 256 * i + 256)
        wide = f[xx].reshape(256, 512).astype(F32)
        fn = jnp.sum(wide * wide, axis=1, keepdims=True) * scale

        def tile(t, carry):
            inner = dot(f[xx].reshape(256, 512), ct[t])
            low = jnp.exp2((2.0 * scale) * inner - (fn + cn[t, 0:1])).astype(BF16)
            weighted = kg[xx, t] * low.astype(F32)
            kb[t, here] = low
            wb[t, here] = weighted.astype(BF16)
            rs[i] += (weighted[:, 0:128] + weighted[:, 128:256]) + (weighted[:, 256:384] + weighted[:, 384:512])
            cs[t] += jnp.sum(weighted.reshape(32, 8, 512), axis=0)
            return carry

        lax.fori_loop(first, last, tile, 0)

    c_cg = {}

    def center_out(t):
        column = jnp.sum(cs[t], axis=0, keepdims=True)
        grad = -factor * (column * ct[t].astype(F32) - dot(ft[...], wb[t]))
        cgs[:, t] = grad.astype(BF16).reshape(4, 128, 512)
        for e in (1, 3, 2):
            c_cg[t, e] = send(cgs.at[plus(y, e), t], cgr.at[e - 1, t], dev(yy=plus(y, e)))

    def wait_slots(ref, first, own):
        for j in range(4):
            @pl.when(own != j)
            def _():
                pltpu.make_async_copy(ref.at[j], ref.at[j], rsem.at[first + j]).wait()

    c_ch = {}

    def center_sum(t):
        s = cgs[y, t].astype(F32)
        for e in (1, 3, 2):
            c_cg[t, e].wait_recv()
            s = s + cgr[e - 1, t].astype(F32)
        s = s.reshape(2, 64, 512)
        cgh[t] = s.astype(BF16)
        o_cg[:, t * 512:t * 512 + 512] = jnp.where(h == 0, s[0], s[1])
        c_ch[t] = send(cgh.at[t, 1 - h], cghr.at[t], dev(hh=1 - h))

    def head_sums(i):
        xx = minus(x, ORDER[i])
        here = slice(256 * i, 256 * i + 256)
        low = jnp.concatenate([kb[t, here] for t in range(4)], axis=1)
        rp[i, :, :, 512:] = dot(low, qp[...]).astype(BF16).reshape(2, 128, 128)
        low = jnp.concatenate([wb[t, here] for t in range(4)], axis=1)
        rows = jnp.sum(rs[i], axis=1, keepdims=True)
        fgrad = -factor * (rows * f[xx].reshape(256, 512).astype(F32) - dot(low, ctr[...]))
        rp[i, :, :, :512] = fgrad.astype(BF16).reshape(2, 128, 512)
        c_pair[i] = send(rp.at[i, 1 - k], prv.at[i], sib)

    for e in ORDER:
        c_fp[e].wait_recv()
    for i, d in enumerate(ORDER):
        if i:
            c_fs[d].wait_recv()
        ft[:, 256 * i:256 * i + 256] = f[minus(x, d)].reshape(256, 512).T
        if i < 3:
            weigh(i, 0, 2)
            forward(ORDER[i + 1])
    weigh(3, 0, 1)
    center_out(0)
    weigh(3, 1, 2)
    center_out(1)
    for i in (1, 2, 3, 0):
        weigh(i, 2, 4)
        if i != 1:
            finish_pair((i + 3) % 4)
        head_sums(i)
    r_cf = new("r", 4)
    turned = jnp.concatenate([cott[minus(x, d)] for d in ORDER], axis=1)[0:112]
    for t in range(4):
        cfs[t] = dot(turned, kb[t]).astype(BF16)
    for e in (1, 3, 2):
        send(cfs.at[plus(y, e)], cfr.at[y], dev(yy=plus(y, e)), r_cf + y)
    cfr[y] = cfs[y]
    finish_pair(0)

    total = xown[...]
    for i in (1, 2, 3):
        c_xr[i].wait_recv()
        total = total + xr[i - 1].astype(F32)
    total = total.reshape(4, 32, 640)
    z2own[...] = total
    z2[...] = total.astype(BF16)
    c_z2 = {e: send(z2.at[plus(zl, e)], z2r.at[e - 1], dev(zz=plus(zl, e))) for e in (1, 3, 2)}
    center_out(2)
    center_out(3)
    center_sum(0)
    center_sum(1)
    total = z2own[zl]
    for e in (1, 3, 2):
        c_z2[e].wait_recv()
        total = total + z2r[e - 1].astype(F32)
    o_pred[...] = total[:, 512:612]
    phi = (total[:, :512] * (1.0 - sq[...] * sq[...])).astype(BF16)
    ph[k, zl] = phi
    c_ph = {e: send(ph.at[k, zl], ph.at[k, zl], dev(zz=plus(zl, e))) for e in (1, 3, 2)}
    wait_slots(cfr, r_cf, y)
    s = (cfr[0].astype(F32) + cfr[1].astype(F32)) + (cfr[2].astype(F32) + cfr[3].astype(F32))
    cfh[...] = s.astype(BF16)
    c_cfh = send(cfh, cfhr, dev(hh=1 - h))
    c_phs = []
    for e in ORDER:
        if e:
            c_ph[e].wait_recv()
        piece = ph.at[k, minus(zl, e)]
        c_phs.append(send(piece, piece, sib))
    for cp in c_phs:
        cp.wait_recv()

    phi_all = ph[...].reshape(256, 512)
    hgrad = lax.dot_general(phi_all, sg[...].reshape(256, 512), (((1,), (1,)), ((), ())), preferred_element_type=F32)
    pgrad = hgrad * gd[...]
    bias_grad = jnp.sum(pgrad, axis=0, keepdims=True)
    plow = pgrad.astype(BF16)
    phit = phi_all.T
    bias_rows = jnp.broadcast_to(bias_grad, (16, 256)).astype(BF16)
    second_grad = dot(phit, hid[...]).astype(BF16)
    for yy in range(4):
        for hh in range(2):
            q = 2 * yy + hh
            grad = dot(gt[q], plow).astype(BF16)
            tt[yy, hh] = grad[0:192]
            rest = jnp.concatenate([grad[192:256], second_grad[64 * q:64 * q + 64], bias_rows], axis=0)
            tb[0, hh, yy] = rest[:, :128]
            tb[1, hh, yy] = rest[:, 128:]

    def to_units(source, target, first):
        for j in range(2):
            for hh in range(2):
                sid = new("s")
                mine = jnp.logical_and(x == 2 * k + j, k == hh)
                src, dst, rid = source.at[j, hh], target.at[x], first + x
                x_sends.append((src, sid, mine))

                @pl.when(mine)
                def _():
                    pltpu.make_async_copy(src, dst, rsem.at[rid]).start()

                @pl.when(jnp.logical_not(mine))
                def _():
                    remote(src, dst, dev(xx=2 * k + j, kk=hh), sid, rid).start()

    def wait_units(ref, first):
        for j in range(4):
            pltpu.make_async_copy(ref.at[j], ref.at[j], rsem.at[first + j]).wait()

    x_sends = []
    r_vb = new("r", 4)
    to_units(tb, vb, r_vb)
    r_t = new("r", 4)
    for e in (2, 1, 3):
        send(tt.at[plus(y, e)], tr.at[y], dev(yy=plus(y, e)), r_t + y)
    tr[y] = tt[y]
    wait_units(vb, r_vb)
    s = (vb[0].astype(F32) + vb[1].astype(F32)) + (vb[2].astype(F32) + vb[3].astype(F32))
    ub[...] = s.astype(BF16)
    r_w2 = new("r", 4)
    for e in (2, 1, 3):
        send(ub.at[plus(y, e)], yb.at[y], dev(yy=plus(y, e)), r_w2 + y)
    yb[y] = ub[y]

    center_sum(2)
    center_sum(3)

    wait_slots(tr, r_t, y)
    for hh in range(2):
        s = (tr[0, hh].astype(F32) + tr[1, hh].astype(F32)) + (tr[2, hh].astype(F32) + tr[3, hh].astype(F32))
        low = s.astype(BF16)
        u[0, hh] = low[:, :128]
        u[1, hh] = low[:, 128:]
    r_v = new("r", 4)
    to_units(u, v, r_v)

    c_cfh.wait_recv()
    o_coef[y] = (cfh[...].astype(F32) + cfhr[...].astype(F32)).astype(BF16)
    r_o = new("r", 4)
    for e in (1, 3, 2):
        send(o_coef.at[y], o_coef.at[y], dev(yy=plus(y, e)), r_o + y)

    wait_slots(yb, r_w2, y)
    s = (yb[0].astype(F32) + yb[1].astype(F32)) + (yb[2].astype(F32) + yb[3].astype(F32))
    mix[192:336] = s
    mix[336:384] = jnp.zeros((48, 128), F32)
    wait_units(v, r_v)
    mix[0:192] = (v[0].astype(F32) + v[1].astype(F32)) + (v[2].astype(F32) + v[3].astype(F32))
    hs[...] = mix[...].T.astype(BF16).reshape(2, 64, 384)
    s_across, s_also, r_across, s_last, r_last = new("s"), new("s"), new("r"), new("s"), new("r")

    @pl.when(k != h)
    def _():
        remote(hs.at[k], hb, dev(hh=1 - h, kk=k), s_across, r_across).start()
        remote(hs.at[1 - k], hb, dev(hh=1 - h, kk=1 - k), s_also, r_across).start()

    @pl.when(k == h)
    def _():
        remote(hs.at[1 - k], ha, sib, s_last, r_last).start()

    for t in range(4):
        c_ch[t].wait_recv()
        o_cg[:, t * 512:t * 512 + 512] += cghr[t].astype(F32)

    @pl.when(k == h)
    def _():
        ha[...] = hs[k]

    @pl.when(k != h)
    def _():
        pltpu.make_async_copy(ha, ha, rsem.at[r_last]).wait()

    pltpu.make_async_copy(hb, hb, rsem.at[r_across]).wait()
    tot = ha[...].astype(F32) + hb[...].astype(F32)
    o_first[...] = tot[:, 0:256]
    o_second[...] = tot[:, 256:320]
    o_bias[...] = tot[:, 256:384].T[64:65]
    wait_slots(o_coef, r_o, y)

    for cp in sent:
        cp.wait_send()
    for src, dst, sid in homes:
        @pl.when(k != x // 2)
        def _():
            pltpu.make_async_copy(src, src, ssem.at[sid]).wait()
    for src, sid, mine in x_sends:
        @pl.when(jnp.logical_not(mine))
        def _():
            pltpu.make_async_copy(src, src, ssem.at[sid]).wait()

    @pl.when(k != h)
    def _():
        pltpu.make_async_copy(ha, ha, ssem.at[s_across]).wait()
        pltpu.make_async_copy(ha, ha, ssem.at[s_also]).wait()

    @pl.when(k == h)
    def _():
        pltpu.make_async_copy(ha, ha, ssem.at[s_last]).wait()


SCRATCH = (
    ("embt", (64, 1024), BF16), ("w1t", (64, 1024), BF16), ("ctr", (2048, 512), BF16), ("coeft", (100, 2048), BF16), ("cott_in", (100, 1024), BF16),
    ("emb_sib", (64, 1024), BF16), ("emb_all", (4, 4, 2, 32, 128), BF16), ("w_sib", (64, 1024), BF16),
    ("w_pair", (2, 512, 128), BF16), ("b_mine", (8, 128), F32), ("b_sib", (8, 128), F32), ("b_pair", (8, 128), F32),
    ("wg", (2, 4, 512, 128), BF16), ("sg", (2, 2, 64, 512), BF16), ("bg", (2, 2, 8, 128), F32),
    ("g", (4, 4, 2, 4, 32, 128), BF16), ("gt", (8, 256, 256), BF16),
    ("hid", (256, 256), BF16), ("gd", (256, 256), F32),
    ("part", (2, 128, 512), F32), ("part_in", (128, 512), F32),
    ("zs", (4, 32, 512), BF16), ("zown", (4, 32, 512), F32), ("zr", (3, 32, 512), BF16), ("sq", (32, 512), F32),
    ("f", (4, 2, 4, 32, 512), BF16), ("ft", (512, 1024), BF16), ("ct", (4, 512, 512), BF16),
    ("qp", (2048, 128), BF16), ("qt", (4, 128, 512), BF16), ("cn", (4, 8, 512), F32),
    ("cot_pad", (128, 1024), BF16), ("cot_all", (4, 4, 2, 32, 128), BF16), ("cotp", (4, 256, 128), BF16), ("cott", (4, 128, 256), BF16),
    ("kg", (4, 4, 256, 512), F32), ("kb", (4, 1024, 512), BF16), ("wb", (4, 1024, 512), BF16),
    ("rs", (4, 256, 128), F32), ("cs", (4, 8, 512), F32),
    ("rp", (4, 2, 128, 640), BF16), ("prv", (4, 128, 640), BF16), ("xown", (128, 640), F32),
    ("xs_out", (3, 128, 640), BF16), ("xr", (3, 128, 640), BF16),
    ("z2", (4, 32, 640), BF16), ("z2own", (4, 32, 640), F32), ("z2r", (3, 32, 640), BF16), ("ph", (2, 4, 32, 512), BF16),
    ("cgs", (4, 4, 128, 512), BF16), ("cgr", (3, 4, 128, 512), BF16), ("cgh", (4, 2, 64, 512), BF16), ("cghr", (4, 64, 512), BF16),
    ("cfs", (4, 112, 512), BF16), ("cfr", (4, 112, 512), BF16), ("cfh", (112, 512), BF16), ("cfhr", (112, 512), BF16),
    ("tt", (4, 2, 192, 256), BF16), ("tr", (4, 2, 192, 256), BF16), ("u", (2, 2, 192, 128), BF16), ("v", (4, 192, 128), BF16),
    ("tb", (2, 2, 4, 144, 128), BF16), ("vb", (4, 4, 144, 128), BF16), ("ub", (4, 144, 128), BF16), ("yb", (4, 144, 128), BF16),
    ("mix", (384, 128), F32), ("hs", (2, 64, 384), BF16), ("ha", (64, 384), BF16), ("hb", (64, 384), BF16),
)


def finish(pred, first, second, bias, cg, coef, o_pred, o_first, o_second, o_bias, o_cg, o_coef):
    o_pred[...] = pred[...]
    o_first[...] = first[...]
    o_second[...] = second[...]
    o_bias[...] = bias[...]
    o_cg[...] = cg[...]
    for t in range(4):
        o_coef[:, t * 512:t * 512 + 512] = coef[t, 0:100].astype(F32)


def body(embeddings, first_weight, first_bias, second_weight, centers, coefficients, cotangent):
    args = (
        embeddings.T,
        first_weight.T,
        first_bias.reshape(1, 64),
        second_weight,
        centers,
        coefficients.T,
        cotangent.T,
    )
    vmem = pl.BlockSpec(memory_space=pltpu.VMEM)
    anywhere = pl.BlockSpec(memory_space=pl.ANY)
    outs = (
        jax.ShapeDtypeStruct((32, 100), F32),
        jax.ShapeDtypeStruct((64, 256), F32),
        jax.ShapeDtypeStruct((64, 64), F32),
        jax.ShapeDtypeStruct((1, 64), F32),
        jax.ShapeDtypeStruct((64, 2048), F32),
        jax.ShapeDtypeStruct((4, 112, 512), BF16),
    )
    made = pl.pallas_call(
        kernel,
        out_shape=outs,
        in_specs=[anywhere, anywhere, vmem, anywhere, anywhere, anywhere, anywhere],
        out_specs=[vmem] * len(outs),
        scratch_shapes=[pltpu.VMEM(shape, dtype) for name, shape, dtype in SCRATCH]
        + [pltpu.SemaphoreType.DMA((SEMS,)), pltpu.SemaphoreType.DMA((SEMS,))],
        compiler_params=pltpu.CompilerParams(collective_id=0, has_side_effects=True, vmem_limit_bytes=60 << 20),
        name="layer",
    )(*args)
    predictions, grad_first, grad_second, grad_bias, grad_centers, grad_coefs = pl.pallas_call(
        finish,
        out_shape=outs[:5] + (jax.ShapeDtypeStruct((100, 2048), F32),),
        in_specs=[vmem] * len(outs),
        out_specs=[vmem] * len(outs),
        name="finish",
    )(*made)
    return (predictions, grad_first.T, grad_bias[0], grad_second, grad_centers.T, grad_coefs.T)


def solution(mesh):
    placed = (
        P("dp", "center"),
        P(None, "center"),
        P("center"),
        P("center", None),
        P("center", None),
        P("center", None),
        P("dp", None),
    )
    return jax.shard_map(
        body,
        mesh=mesh,
        in_specs=placed,
        out_specs=(
            P(("dp", "center"), None),
            P("dp", "center"),
            P("center"),
            P("center", "dp"),
            P("center", "dp"),
            P("center", None),
        ),
        check_vma=False,
    )
```

```python
import functools
import math

import jax
import jax.numpy as jnp
from jax import lax
from jax.experimental import pallas as pl
from jax.experimental.pallas import tpu as pltpu
from jax.sharding import PartitionSpec as P

MESH = pl.DeviceIdType.MESH
F32 = jnp.float32
BF16 = jnp.bfloat16
ORDER = (0, 1, 3, 2)
GELU_C = math.sqrt(2.0 / math.pi)
LOG2E = math.log2(math.e)
SEMS = 160


def dot(a, b):
    return jnp.dot(a, b, preferred_element_type=F32)


def kernel(embt_hbm, w1t_hbm, b1, w2, ctr_hbm, coeft_hbm, cott_hbm,
           o_pred, o_first, o_second, o_bias, o_cg, o_coef,
           embt, w1t, ctr, coeft, cott_in, emb_sib, emb_all, w_sib, w_pair, b_mine, b_sib, b_pair, wg, sg, bg, g, gt,
           hid, gd, part, part_in, zs, zown, zr, sq, f, ft, ct,
           qp, qt, cn, cot_pad, cot_all, cotp, cott, kg, kb, wb,
           rs, cs, rp, prv, xown, xs_out, xr, z2, z2own, z2r, ph,
           cgs, cgr, cgh, cghr, cfs, cfr, cfh, cfo, cfhr, tt, tr, u, v, tb, vb, ub, yb, mix, hs, ha, hb,
           ssem, rsem):
    dp = lax.axis_index("dp")
    c = lax.axis_index("center")
    y, h = dp // 2, dp % 2
    zl, x, k = c // 8, (c // 2) % 4, c % 2
    feat = 512
    factor = 16.0 / feat
    scale = 8.0 / feat * LOG2E

    def dev(xx=None, yy=None, hh=None, zz=None, kk=None):
        xx = x if xx is None else xx
        yy = y if yy is None else yy
        hh = h if hh is None else hh
        zz = zl if zz is None else zz
        kk = k if kk is None else kk
        return {"dp": yy * 2 + hh, "center": zz * 8 + xx * 2 + kk}

    def plus(a, d):
        return lax.rem(a + d, 4)

    def minus(a, d):
        return lax.rem(a + 4 - d, 4)

    ids = {"s": 0, "r": 0}
    sent = []

    def new(kind, n=1):
        first = ids[kind]
        ids[kind] += n
        assert ids[kind] <= SEMS
        return first

    def remote(src, dst, target, sid, rid):
        return pltpu.make_async_remote_copy(
            src_ref=src, dst_ref=dst, send_sem=ssem.at[sid], recv_sem=rsem.at[rid],
            device_id=target, device_id_type=MESH)

    def send(src, dst, target, rid=None):
        rid = new("r") if rid is None else rid
        cp = remote(src, dst, target, new("s"), rid)
        cp.start()
        sent.append(cp)
        return cp

    def to_home(src, dst_at, rid_at):
        rid = rid_at
        for d in (1, 3, 2):
            send(src, dst_at, dev(xx=plus(x, d), kk=x // 2), rid)
        sid = new("s")

        @pl.when(k == x // 2)
        def _():
            pltpu.make_async_copy(src, dst_at, rsem.at[rid]).start()

        @pl.when(k != x // 2)
        def _():
            remote(src, dst_at, dev(kk=1 - k), sid, rid).start()
        homes.append((src, dst_at, sid))

    homes = []

    barrier = pltpu.get_barrier_semaphore()
    peers = [dev(kk=1 - k), dev(hh=1 - h), dev(hh=1 - h, kk=1 - k)]
    for d in (1, 2, 3):
        peers += [dev(xx=plus(x, d)), dev(xx=plus(x, d), kk=1 - k), dev(zz=plus(zl, d)), dev(yy=plus(y, d))]
    for peer in peers:
        pl.semaphore_signal(barrier, inc=1, device_id=peer, device_id_type=MESH)
    loads = []
    own_half = pl.ds(pl.multiple_of(k * 1024, 1024), 1024)
    for src, dst in ((embt_hbm, embt), (w1t_hbm.at[:, own_half], w1t), (cott_hbm, cott_in), (coeft_hbm, coeft), (ctr_hbm, ctr)):
        loads.append(pltpu.make_async_copy(src, dst, rsem.at[new("r")]))
        loads[-1].start()
    wide_bias = jnp.broadcast_to(b1[...], (8, 64))
    b_mine[...] = jnp.concatenate([wide_bias, wide_bias], axis=1)
    pl.semaphore_wait(barrier, len(peers))
    sib = dev(kk=1 - k)

    c_emb = send(embt_hbm, emb_sib, sib)
    c_w = send(w1t_hbm.at[:, pl.ds(pl.multiple_of((1 - k) * 1024, 1024), 1024)], w_sib, sib)
    c_b = send(b_mine, b_sib, sib)

    def paired(mine, other):
        low = jnp.where(k == 0, mine, other)
        high = jnp.where(k == 0, other, mine)
        return jnp.concatenate([low, high], axis=0)

    loads[0].wait()
    c_emb.wait_recv()
    emb_all[...] = paired(embt[...], emb_sib[...]).T.reshape(4, 4, 2, 32, 128)
    c_x = {}
    for d in (1, 3, 2):
        c_x[d] = send(emb_all.at[:, plus(x, d), k], g.at[zl, x, k], dev(xx=plus(x, d)))
    g[zl, x, k] = emb_all[:, x, k]

    loads[1].wait()
    c_w.wait_recv()
    w_pair[...] = paired(w1t[...], w_sib[...]).T.reshape(2, 512, 128)
    r_w = new("r", 4)
    to_home(w_pair, wg.at[x % 2, pl.ds(2 * k, 2)], r_w + 2 * (x % 2) + k)
    c_b.wait_recv()
    lane = lax.broadcasted_iota(jnp.int32, (8, 128), 1)
    b_pair[...] = jnp.where((lane < 64) == (k == 0), b_mine[...], b_sib[...])
    r_b = new("r", 4)
    to_home(b_pair, bg.at[x % 2, k], r_b + 2 * (x % 2) + k)

    r_sg = new("r", 4)
    to_home(w2, sg.at[x % 2, k], r_sg + 2 * (x % 2) + k)

    c_z = {}
    for d in ORDER:
        xx = minus(x, d)
        if d:
            c_x[d].wait_recv()
        piece = g.at[zl, xx, k]
        for e in (1, 3, 2):
            c_z[d, e] = send(piece, piece, dev(zz=plus(zl, e)))
    c_gs = {0: send(g.at[zl, :, k], g.at[zl, :, k], sib)}

    for load in loads[2:]:
        load.wait()
    cot_pad[...] = jnp.zeros_like(cot_pad)
    cot_pad[0:100] = cott_in[...]
    cot_all[...] = cot_pad[...].T.reshape(4, 4, 2, 32, 128)
    for xx in range(4):
        for kk in range(2):
            cotp[xx, kk * 128:kk * 128 + 128] = cot_all[:, xx, kk].reshape(128, 128)
        cott[xx] = cotp[xx].T
    qt[...] = jnp.zeros_like(qt)
    for t in range(4):
        qt[t, 0:100] = coeft[:, t * 512:t * 512 + 512]

    def prepare(t, carry):
        rows = pl.ds(pl.multiple_of(t * 512, 512), 512)
        qp[rows] = qt[t].T
        turned = ctr[rows].T
        ct[t] = turned
        wide = turned.astype(F32)
        cn[t] = jnp.broadcast_to(jnp.sum(wide * wide, axis=0, keepdims=True) * scale, (8, 512))
        cs[t] = jnp.zeros((8, 512), F32)
        rs[t] = jnp.zeros((256, 128), F32)
        for xx in range(4):
            kg[xx, t] = dot(cotp[xx], qt[t])
        return carry

    lax.fori_loop(0, 4, prepare, 0)

    def wait_home(ref, first):
        for i in range(2):
            for j in range(2):
                pltpu.make_async_copy(ref.at[i, pl.ds(2 * j, 2)] if ref is wg else ref.at[i, j],
                                      ref.at[i, pl.ds(2 * j, 2)] if ref is wg else ref.at[i, j],
                                      rsem.at[first + 2 * i + j]).wait()

    wait_home(wg, r_w)

    acc = jnp.zeros((256, 256), F32)
    for n, e in enumerate(ORDER):
        src = minus(zl, e)
        if n < 3:
            nxt = ORDER[n + 1]
            for d in ORDER:
                c_z[d, nxt].wait_recv()
            c_gs[nxt] = send(g.at[minus(zl, nxt), :, k], g.at[minus(zl, nxt), :, k], sib)
        c_gs[e].wait_recv()
        lhs = jnp.concatenate([g[src, xx].reshape(256, 128) for xx in range(4)], axis=1)
        rhs = jnp.concatenate([wg[0, src], wg[1, src]], axis=1)
        acc = acc + dot(lhs, rhs)
    wait_home(bg, r_b)
    wait_home(sg, r_sg)
    bias = jnp.concatenate([bg[0, 0], bg[1, 0]], axis=1)[0:1]
    u0 = acc + bias
    t0 = jnp.tanh(GELU_C * (u0 + 0.044715 * (u0 * u0 * u0)))
    hid[...] = (u0 * (0.5 * (1.0 + t0))).astype(BF16)
    second = sg[...].reshape(256, 512)
    part[...] = dot(hid[...], second).reshape(2, 128, 512)
    c_p = send(part.at[1 - k], part_in, sib)
    gd[...] = 0.5 * (1.0 + t0) + 0.5 * u0 * (1.0 - t0 * t0) * (GELU_C * (1.0 + 3.0 * 0.044715 * (u0 * u0)))
    c_p.wait_recv()
    summed = (part[k] + part_in[...]).reshape(4, 32, 512)
    zown[...] = summed
    zs[...] = summed.astype(BF16)
    c_f = {}
    for e in (1, 3, 2):
        c_f[e] = send(zs.at[plus(zl, e)], zr.at[e - 1], dev(zz=plus(zl, e)))
    for zz in range(4):
        for xx in range(4):
            gt[zz * 2 + xx // 2, pl.ds((xx % 2) * 128, 128)] = g[zz, xx].reshape(256, 128).T
    total = zown[zl]
    for e in (1, 3, 2):
        c_f[e].wait_recv()
        total = total + zr[e - 1].astype(F32)
    squashed = jnp.tanh(total)
    sq[...] = squashed
    f[x, k, zl] = squashed.astype(BF16)

    own_piece = f.at[x, k, zl]
    c_fz = {e: send(own_piece, own_piece, dev(zz=plus(zl, e))) for e in (1, 3, 2)}
    c_fx = {}
    c_fp = {}
    for e in ORDER:
        if e:
            c_fz[e].wait_recv()
        piece = f.at[x, k, minus(zl, e)]
        c_fp[e] = send(piece, piece, sib)
        for d in (1, 3, 2):
            c_fx[d, e] = send(piece, piece, dev(xx=plus(x, d)))
    c_fs = {}

    def forward(d):
        for e in ORDER:
            c_fx[d, e].wait_recv()
        block = f.at[minus(x, d), k]
        c_fs[d] = send(block, block, sib)

    c_pair = {}
    c_xr = {}

    def finish_pair(i):
        c_pair[i].wait_recv()
        both = rp[i, k].astype(F32) + prv[i].astype(F32)
        if i == 0:
            xown[...] = both
        else:
            xs_out[i - 1] = both.astype(BF16)
            c_xr[i] = send(xs_out.at[i - 1], xr.at[i - 1], dev(xx=minus(x, ORDER[i])))

    def weigh(i, first, last):
        xx = minus(x, ORDER[i])
        here = slice(256 * i, 256 * i + 256)
        wide = f[xx].reshape(256, 512).astype(F32)
        fn = jnp.sum(wide * wide, axis=1, keepdims=True) * scale

        def tile(t, carry):
            inner = dot(f[xx].reshape(256, 512), ct[t])
            low = jnp.exp2((2.0 * scale) * inner - (fn + cn[t, 0:1])).astype(BF16)
            weighted = kg[xx, t] * low.astype(F32)
            kb[t, here] = low
            wb[t, here] = weighted.astype(BF16)
            rs[i] += (weighted[:, 0:128] + weighted[:, 128:256]) + (weighted[:, 256:384] + weighted[:, 384:512])
            cs[t] += jnp.sum(weighted.reshape(32, 8, 512), axis=0)
            return carry

        lax.fori_loop(first, last, tile, 0)

    c_cg = {}

    def center_out(t):
        column = jnp.sum(cs[t], axis=0, keepdims=True)
        grad = -factor * (column * ct[t].astype(F32) - dot(ft[...], wb[t]))
        cgs[:, t] = grad.astype(BF16).reshape(4, 128, 512)
        for e in (1, 3, 2):
            c_cg[t, e] = send(cgs.at[plus(y, e), t], cgr.at[e - 1, t], dev(yy=plus(y, e)))

    def wait_slots(ref, first, own):
        for j in range(4):
            @pl.when(own != j)
            def _():
                pltpu.make_async_copy(ref.at[j], ref.at[j], rsem.at[first + j]).wait()

    c_ch = {}

    def center_sum(t):
        s = cgs[y, t].astype(F32)
        for e in (1, 3, 2):
            c_cg[t, e].wait_recv()
            s = s + cgr[e - 1, t].astype(F32)
        s = s.reshape(2, 64, 512)
        cgh[t] = s.astype(BF16)
        o_cg[:, t * 512:t * 512 + 512] = jnp.where(h == 0, s[0], s[1])
        c_ch[t] = send(cgh.at[t, 1 - h], cghr.at[t], dev(hh=1 - h))

    def head_sums(i):
        xx = minus(x, ORDER[i])
        here = slice(256 * i, 256 * i + 256)
        low = jnp.concatenate([kb[t, here] for t in range(4)], axis=1)
        rp[i, :, :, 512:] = dot(low, qp[...]).astype(BF16).reshape(2, 128, 128)
        low = jnp.concatenate([wb[t, here] for t in range(4)], axis=1)
        rows = jnp.sum(rs[i], axis=1, keepdims=True)
        fgrad = -factor * (rows * f[xx].reshape(256, 512).astype(F32) - dot(low, ctr[...]))
        rp[i, :, :, :512] = fgrad.astype(BF16).reshape(2, 128, 512)
        c_pair[i] = send(rp.at[i, 1 - k], prv.at[i], sib)

    for e in ORDER:
        c_fp[e].wait_recv()
    for i, d in enumerate(ORDER):
        if i:
            c_fs[d].wait_recv()
        ft[:, 256 * i:256 * i + 256] = f[minus(x, d)].reshape(256, 512).T
        if i < 3:
            weigh(i, 0, 2)
            forward(ORDER[i + 1])
    weigh(3, 0, 1)
    center_out(0)
    weigh(3, 1, 2)
    center_out(1)
    for i in (1, 2, 3, 0):
        weigh(i, 2, 4)
        if i != 1:
            finish_pair((i + 3) % 4)
        head_sums(i)
    r_cf = new("r", 4)
    turned = jnp.concatenate([cott[minus(x, d)] for d in ORDER], axis=1)[0:112]
    for t in range(4):
        cfs[t] = dot(turned, kb[t]).astype(BF16)
    for e in (1, 3, 2):
        send(cfs.at[plus(y, e)], cfr.at[y], dev(yy=plus(y, e)), r_cf + y)
    cfr[y] = cfs[y]
    finish_pair(0)

    total = xown[...]
    for i in (1, 2, 3):
        c_xr[i].wait_recv()
        total = total + xr[i - 1].astype(F32)
    total = total.reshape(4, 32, 640)
    z2own[...] = total
    z2[...] = total.astype(BF16)
    c_z2 = {e: send(z2.at[plus(zl, e)], z2r.at[e - 1], dev(zz=plus(zl, e))) for e in (1, 3, 2)}
    center_out(2)
    center_out(3)
    center_sum(0)
    center_sum(1)
    total = z2own[zl]
    for e in (1, 3, 2):
        c_z2[e].wait_recv()
        total = total + z2r[e - 1].astype(F32)
    o_pred[...] = total[:, 512:612]
    phi = (total[:, :512] * (1.0 - sq[...] * sq[...])).astype(BF16)
    ph[k, zl] = phi
    c_ph = {e: send(ph.at[k, zl], ph.at[k, zl], dev(zz=plus(zl, e))) for e in (1, 3, 2)}
    c_phs = []
    for e in ORDER:
        if e:
            c_ph[e].wait_recv()
        piece = ph.at[k, minus(zl, e)]
        c_phs.append(send(piece, piece, sib))
    for cp in c_phs:
        cp.wait_recv()

    phi_all = ph[...].reshape(256, 512)
    hgrad = lax.dot_general(phi_all, sg[...].reshape(256, 512), (((1,), (1,)), ((), ())), preferred_element_type=F32)
    pgrad = hgrad * gd[...]
    bias_grad = jnp.sum(pgrad, axis=0, keepdims=True)
    plow = pgrad.astype(BF16)
    phit = phi_all.T
    bias_rows = jnp.broadcast_to(bias_grad, (16, 256)).astype(BF16)
    second_grad = dot(phit, hid[...]).astype(BF16)
    for yy in range(4):
        for hh in range(2):
            q = 2 * yy + hh
            grad = dot(gt[q], plow).astype(BF16)
            tt[yy, hh] = grad[0:192]
            rest = jnp.concatenate([grad[192:256], second_grad[64 * q:64 * q + 64], bias_rows], axis=0)
            tb[0, hh, yy] = rest[:, :128]
            tb[1, hh, yy] = rest[:, 128:]

    def to_units(source, target, first):
        for j in range(2):
            for hh in range(2):
                sid = new("s")
                mine = jnp.logical_and(x == 2 * k + j, k == hh)
                src, dst, rid = source.at[j, hh], target.at[x], first + x
                x_sends.append((src, sid, mine))

                @pl.when(mine)
                def _():
                    pltpu.make_async_copy(src, dst, rsem.at[rid]).start()

                @pl.when(jnp.logical_not(mine))
                def _():
                    remote(src, dst, dev(xx=2 * k + j, kk=hh), sid, rid).start()

    def wait_units(ref, first):
        for j in range(4):
            pltpu.make_async_copy(ref.at[j], ref.at[j], rsem.at[first + j]).wait()

    x_sends = []
    r_vb = new("r", 4)
    to_units(tb, vb, r_vb)
    r_t = new("r", 4)
    for e in (2, 1, 3):
        send(tt.at[plus(y, e)], tr.at[y], dev(yy=plus(y, e)), r_t + y)
    tr[y] = tt[y]
    wait_slots(cfr, r_cf, y)
    s = (cfr[0].astype(F32) + cfr[1].astype(F32)) + (cfr[2].astype(F32) + cfr[3].astype(F32))
    cfh[...] = s.astype(BF16)
    c_cfh = send(cfh, cfhr, dev(hh=1 - h))
    wait_units(vb, r_vb)
    s = (vb[0].astype(F32) + vb[1].astype(F32)) + (vb[2].astype(F32) + vb[3].astype(F32))
    ub[...] = s.astype(BF16)
    r_w2 = new("r", 4)
    for e in (2, 1, 3):
        send(ub.at[plus(y, e)], yb.at[y], dev(yy=plus(y, e)), r_w2 + y)
    yb[y] = ub[y]

    center_sum(2)
    center_sum(3)

    wait_slots(tr, r_t, y)
    for hh in range(2):
        s = (tr[0, hh].astype(F32) + tr[1, hh].astype(F32)) + (tr[2, hh].astype(F32) + tr[3, hh].astype(F32))
        low = s.astype(BF16)
        u[0, hh] = low[:, :128]
        u[1, hh] = low[:, 128:]
    r_v = new("r", 4)
    to_units(u, v, r_v)

    c_cfh.wait_recv()
    cfo[y] = (cfh[...].astype(F32) + cfhr[...].astype(F32)).astype(BF16)
    r_o = new("r", 4)
    for e in (1, 3, 2):
        send(cfo.at[y], cfo.at[y], dev(yy=plus(y, e)), r_o + y)

    wait_slots(yb, r_w2, y)
    s = (yb[0].astype(F32) + yb[1].astype(F32)) + (yb[2].astype(F32) + yb[3].astype(F32))
    mix[192:336] = s
    mix[336:384] = jnp.zeros((48, 128), F32)
    wait_units(v, r_v)
    mix[0:192] = (v[0].astype(F32) + v[1].astype(F32)) + (v[2].astype(F32) + v[3].astype(F32))
    hs[...] = mix[...].T.astype(BF16).reshape(2, 64, 384)
    s_across, s_also, r_across, s_last, r_last = new("s"), new("s"), new("r"), new("s"), new("r")

    @pl.when(k != h)
    def _():
        remote(hs.at[k], hb, dev(hh=1 - h, kk=k), s_across, r_across).start()
        remote(hs.at[1 - k], hb, dev(hh=1 - h, kk=1 - k), s_also, r_across).start()

    @pl.when(k == h)
    def _():
        remote(hs.at[1 - k], ha, sib, s_last, r_last).start()

    for t in range(4):
        c_ch[t].wait_recv()
        o_cg[:, t * 512:t * 512 + 512] += cghr[t].astype(F32)

    wait_slots(cfo, r_o, y)
    for t in range(4):
        o_coef[:, t * 512:t * 512 + 512] = cfo[t, 0:100].astype(F32)

    @pl.when(k == h)
    def _():
        ha[...] = hs[k]

    @pl.when(k != h)
    def _():
        pltpu.make_async_copy(ha, ha, rsem.at[r_last]).wait()

    pltpu.make_async_copy(hb, hb, rsem.at[r_across]).wait()
    tot = ha[...].astype(F32) + hb[...].astype(F32)
    o_first[...] = tot[:, 0:256]
    o_second[...] = tot[:, 256:320]
    o_bias[...] = tot[:, 256:384].T[64:65]

    for cp in sent:
        cp.wait_send()
    for src, dst, sid in homes:
        @pl.when(k != x // 2)
        def _():
            pltpu.make_async_copy(src, src, ssem.at[sid]).wait()
    for src, sid, mine in x_sends:
        @pl.when(jnp.logical_not(mine))
        def _():
            pltpu.make_async_copy(src, src, ssem.at[sid]).wait()

    @pl.when(k != h)
    def _():
        pltpu.make_async_copy(ha, ha, ssem.at[s_across]).wait()
        pltpu.make_async_copy(ha, ha, ssem.at[s_also]).wait()

    @pl.when(k == h)
    def _():
        pltpu.make_async_copy(ha, ha, ssem.at[s_last]).wait()


SCRATCH = (
    ("embt", (64, 1024), BF16), ("w1t", (64, 1024), BF16), ("ctr", (2048, 512), BF16), ("coeft", (100, 2048), BF16), ("cott_in", (100, 1024), BF16),
    ("emb_sib", (64, 1024), BF16), ("emb_all", (4, 4, 2, 32, 128), BF16), ("w_sib", (64, 1024), BF16),
    ("w_pair", (2, 512, 128), BF16), ("b_mine", (8, 128), F32), ("b_sib", (8, 128), F32), ("b_pair", (8, 128), F32),
    ("wg", (2, 4, 512, 128), BF16), ("sg", (2, 2, 64, 512), BF16), ("bg", (2, 2, 8, 128), F32),
    ("g", (4, 4, 2, 4, 32, 128), BF16), ("gt", (8, 256, 256), BF16),
    ("hid", (256, 256), BF16), ("gd", (256, 256), F32),
    ("part", (2, 128, 512), F32), ("part_in", (128, 512), F32),
    ("zs", (4, 32, 512), BF16), ("zown", (4, 32, 512), F32), ("zr", (3, 32, 512), BF16), ("sq", (32, 512), F32),
    ("f", (4, 2, 4, 32, 512), BF16), ("ft", (512, 1024), BF16), ("ct", (4, 512, 512), BF16),
    ("qp", (2048, 128), BF16), ("qt", (4, 128, 512), BF16), ("cn", (4, 8, 512), F32),
    ("cot_pad", (128, 1024), BF16), ("cot_all", (4, 4, 2, 32, 128), BF16), ("cotp", (4, 256, 128), BF16), ("cott", (4, 128, 256), BF16),
    ("kg", (4, 4, 256, 512), F32), ("kb", (4, 1024, 512), BF16), ("wb", (4, 1024, 512), BF16),
    ("rs", (4, 256, 128), F32), ("cs", (4, 8, 512), F32),
    ("rp", (4, 2, 128, 640), BF16), ("prv", (4, 128, 640), BF16), ("xown", (128, 640), F32),
    ("xs_out", (3, 128, 640), BF16), ("xr", (3, 128, 640), BF16),
    ("z2", (4, 32, 640), BF16), ("z2own", (4, 32, 640), F32), ("z2r", (3, 32, 640), BF16), ("ph", (2, 4, 32, 512), BF16),
    ("cgs", (4, 4, 128, 512), BF16), ("cgr", (3, 4, 128, 512), BF16), ("cgh", (4, 2, 64, 512), BF16), ("cghr", (4, 64, 512), BF16),
    ("cfs", (4, 112, 512), BF16), ("cfr", (4, 112, 512), BF16), ("cfh", (112, 512), BF16), ("cfo", (4, 112, 512), BF16), ("cfhr", (112, 512), BF16),
    ("tt", (4, 2, 192, 256), BF16), ("tr", (4, 2, 192, 256), BF16), ("u", (2, 2, 192, 128), BF16), ("v", (4, 192, 128), BF16),
    ("tb", (2, 2, 4, 144, 128), BF16), ("vb", (4, 4, 144, 128), BF16), ("ub", (4, 144, 128), BF16), ("yb", (4, 144, 128), BF16),
    ("mix", (384, 128), F32), ("hs", (2, 64, 384), BF16), ("ha", (64, 384), BF16), ("hb", (64, 384), BF16),
)


def finish(*refs):
    n = len(refs) // 2
    for i in range(n):
        refs[n + i][...] = refs[i][...]


def body(embeddings, first_weight, first_bias, second_weight, centers, coefficients, cotangent):
    args = (
        embeddings.T,
        first_weight.T,
        first_bias.reshape(1, 64),
        second_weight,
        centers,
        coefficients.T,
        cotangent.T,
    )
    vmem = pl.BlockSpec(memory_space=pltpu.VMEM)
    anywhere = pl.BlockSpec(memory_space=pl.ANY)
    outs = (
        jax.ShapeDtypeStruct((32, 100), F32),
        jax.ShapeDtypeStruct((64, 256), F32),
        jax.ShapeDtypeStruct((64, 64), F32),
        jax.ShapeDtypeStruct((1, 64), F32),
        jax.ShapeDtypeStruct((64, 2048), F32),
        jax.ShapeDtypeStruct((100, 2048), F32),
    )
    made = pl.pallas_call(
        kernel,
        out_shape=outs,
        in_specs=[anywhere, anywhere, vmem, anywhere, anywhere, anywhere, anywhere],
        out_specs=[vmem] * len(outs),
        scratch_shapes=[pltpu.VMEM(shape, dtype) for name, shape, dtype in SCRATCH]
        + [pltpu.SemaphoreType.DMA((SEMS,)), pltpu.SemaphoreType.DMA((SEMS,))],
        compiler_params=pltpu.CompilerParams(collective_id=0, has_side_effects=True, vmem_limit_bytes=60 << 20),
        name="layer",
    )(*args)
    predictions, grad_first, grad_second, grad_bias, grad_centers, grad_coefs = pl.pallas_call(
        finish,
        out_shape=outs,
        in_specs=[vmem] * len(outs),
        out_specs=[vmem] * len(outs),
        name="finish",
    )(*made)
    return (predictions, grad_first.T, grad_bias[0], grad_second, grad_centers.T, grad_coefs.T)


def solution(mesh):
    placed = (
        P("dp", "center"),
        P(None, "center"),
        P("center"),
        P("center", None),
        P("center", None),
        P("center", None),
        P("dp", None),
    )
    return jax.shard_map(
        body,
        mesh=mesh,
        in_specs=placed,
        out_specs=(
            P(("dp", "center"), None),
            P("dp", "center"),
            P("center"),
            P("center", "dp"),
            P("center", "dp"),
            P("center", None),
        ),
        check_vma=False,
    )
```

```python
import functools
import math

import jax
import jax.numpy as jnp
from jax import lax
from jax.experimental import pallas as pl
from jax.experimental.pallas import tpu as pltpu
from jax.sharding import PartitionSpec as P

MESH = pl.DeviceIdType.MESH
F32 = jnp.float32
BF16 = jnp.bfloat16
ORDER = (0, 1, 3, 2)
GELU_C = math.sqrt(2.0 / math.pi)
LOG2E = math.log2(math.e)
SEMS = 160


def dot(a, b):
    return jnp.dot(a, b, preferred_element_type=F32)


def kernel(embt_hbm, w1t_hbm, b1, w2, ctr_hbm, coeft_hbm, cott_hbm,
           o_pred, o_first, o_second, o_bias, o_cg, o_coef,
           embt, w1t, ctr, coeft, cott_in, emb_sib, emb_all, w_sib, w_pair, b_mine, b_sib, b_pair, wg, sg, bg, g, gt,
           hid, gd, part, part_in, zs, zown, zr, sq, f, ft, ct,
           qp, qt, cn, cot_pad, cot_all, cotp, cott, kg, kb, wb,
           rs, cs, rp, prv, xown, xs_out, xr, z2, z2own, z2r, ph,
           cgs, cgr, cgh, cghr, cfs, cfr, cfh, cfo, cfhr, tt, tr, u, v, tb, vb, ub, yb, mix, hs, ha, hb,
           ssem, rsem):
    dp = lax.axis_index("dp")
    c = lax.axis_index("center")
    y, h = dp // 2, dp % 2
    zl, x, k = c // 8, (c // 2) % 4, c % 2
    feat = 512
    factor = 16.0 / feat
    scale = 8.0 / feat * LOG2E

    def dev(xx=None, yy=None, hh=None, zz=None, kk=None):
        xx = x if xx is None else xx
        yy = y if yy is None else yy
        hh = h if hh is None else hh
        zz = zl if zz is None else zz
        kk = k if kk is None else kk
        return {"dp": yy * 2 + hh, "center": zz * 8 + xx * 2 + kk}

    def plus(a, d):
        return lax.rem(a + d, 4)

    def minus(a, d):
        return lax.rem(a + 4 - d, 4)

    ids = {"s": 0, "r": 0}
    sent = []

    def new(kind, n=1):
        first = ids[kind]
        ids[kind] += n
        assert ids[kind] <= SEMS
        return first

    def remote(src, dst, target, sid, rid):
        return pltpu.make_async_remote_copy(
            src_ref=src, dst_ref=dst, send_sem=ssem.at[sid], recv_sem=rsem.at[rid],
            device_id=target, device_id_type=MESH)

    def send(src, dst, target, rid=None):
        rid = new("r") if rid is None else rid
        cp = remote(src, dst, target, new("s"), rid)
        cp.start()
        sent.append(cp)
        return cp

    def to_home(src, dst_at, rid_at):
        rid = rid_at
        for d in (1, 3, 2):
            send(src, dst_at, dev(xx=plus(x, d), kk=x // 2), rid)
        sid = new("s")

        @pl.when(k == x // 2)
        def _():
            pltpu.make_async_copy(src, dst_at, rsem.at[rid]).start()

        @pl.when(k != x // 2)
        def _():
            remote(src, dst_at, dev(kk=1 - k), sid, rid).start()
        homes.append((src, dst_at, sid))

    homes = []

    barrier = pltpu.get_barrier_semaphore()
    peers = [dev(kk=1 - k), dev(hh=1 - h), dev(hh=1 - h, kk=1 - k)]
    for d in (1, 2, 3):
        peers += [dev(xx=plus(x, d)), dev(xx=plus(x, d), kk=1 - k), dev(zz=plus(zl, d)), dev(yy=plus(y, d))]
    for peer in peers:
        pl.semaphore_signal(barrier, inc=1, device_id=peer, device_id_type=MESH)
    loads = []
    own_half = pl.ds(pl.multiple_of(k * 1024, 1024), 1024)
    for src, dst in ((embt_hbm, embt), (w1t_hbm.at[:, own_half], w1t), (cott_hbm, cott_in), (coeft_hbm, coeft), (ctr_hbm, ctr)):
        loads.append(pltpu.make_async_copy(src, dst, rsem.at[new("r")]))
        loads[-1].start()
    wide_bias = jnp.broadcast_to(b1[...], (8, 64))
    b_mine[...] = jnp.concatenate([wide_bias, wide_bias], axis=1)
    pl.semaphore_wait(barrier, len(peers))
    sib = dev(kk=1 - k)

    c_emb = send(embt_hbm, emb_sib, sib)
    c_w = send(w1t_hbm.at[:, pl.ds(pl.multiple_of((1 - k) * 1024, 1024), 1024)], w_sib, sib)
    c_b = send(b_mine, b_sib, sib)

    def paired(mine, other):
        low = jnp.where(k == 0, mine, other)
        high = jnp.where(k == 0, other, mine)
        return jnp.concatenate([low, high], axis=0)

    loads[0].wait()
    c_emb.wait_recv()
    emb_all[...] = paired(embt[...], emb_sib[...]).T.reshape(4, 4, 2, 32, 128)
    c_x = {}
    for d in (1, 3, 2):
        c_x[d] = send(emb_all.at[:, plus(x, d), k], g.at[zl, x, k], dev(xx=plus(x, d)))
    g[zl, x, k] = emb_all[:, x, k]

    loads[1].wait()
    c_w.wait_recv()
    w_pair[...] = paired(w1t[...], w_sib[...]).T.reshape(2, 512, 128)
    r_w = new("r", 4)
    to_home(w_pair, wg.at[x % 2, pl.ds(2 * k, 2)], r_w + 2 * (x % 2) + k)
    c_b.wait_recv()
    lane = lax.broadcasted_iota(jnp.int32, (8, 128), 1)
    b_pair[...] = jnp.where((lane < 64) == (k == 0), b_mine[...], b_sib[...])
    r_b = new("r", 4)
    to_home(b_pair, bg.at[x % 2, k], r_b + 2 * (x % 2) + k)

    r_sg = new("r", 4)
    to_home(w2, sg.at[x % 2, k], r_sg + 2 * (x % 2) + k)

    c_z = {}
    for d in ORDER:
        xx = minus(x, d)
        if d:
            c_x[d].wait_recv()
        piece = g.at[zl, xx, k]
        for e in (1, 3, 2):
            c_z[d, e] = send(piece, piece, dev(zz=plus(zl, e)))
    c_gs = {0: send(g.at[zl, :, k], g.at[zl, :, k], sib)}

    for load in loads[2:]:
        load.wait()
    cot_pad[...] = jnp.zeros_like(cot_pad)
    cot_pad[0:100] = cott_in[...]
    cot_all[...] = cot_pad[...].T.reshape(4, 4, 2, 32, 128)
    for xx in range(4):
        for kk in range(2):
            cotp[xx, kk * 128:kk * 128 + 128] = cot_all[:, xx, kk].reshape(128, 128)
        cott[xx] = cotp[xx].T
    qt[...] = jnp.zeros_like(qt)
    for t in range(4):
        qt[t, 0:100] = coeft[:, t * 512:t * 512 + 512]

    def prepare(t, carry):
        rows = pl.ds(pl.multiple_of(t * 512, 512), 512)
        qp[rows] = qt[t].T
        turned = ctr[rows].T
        ct[t] = turned
        wide = turned.astype(F32)
        cn[t] = jnp.broadcast_to(jnp.sum(wide * wide, axis=0, keepdims=True) * scale, (8, 512))
        cs[t] = jnp.zeros((8, 512), F32)
        rs[t] = jnp.zeros((256, 128), F32)
        for xx in range(4):
            kg[xx, t] = dot(cotp[xx], qt[t])
        return carry

    lax.fori_loop(0, 4, prepare, 0)

    def wait_home(ref, first):
        for i in range(2):
            for j in range(2):
                pltpu.make_async_copy(ref.at[i, pl.ds(2 * j, 2)] if ref is wg else ref.at[i, j],
                                      ref.at[i, pl.ds(2 * j, 2)] if ref is wg else ref.at[i, j],
                                      rsem.at[first + 2 * i + j]).wait()

    wait_home(wg, r_w)

    acc = jnp.zeros((256, 256), F32)
    for n, e in enumerate(ORDER):
        src = minus(zl, e)
        if n < 3:
            nxt = ORDER[n + 1]
            for d in ORDER:
                c_z[d, nxt].wait_recv()
            c_gs[nxt] = send(g.at[minus(zl, nxt), :, k], g.at[minus(zl, nxt), :, k], sib)
        c_gs[e].wait_recv()
        lhs = jnp.concatenate([g[src, xx].reshape(256, 128) for xx in range(4)], axis=1)
        rhs = jnp.concatenate([wg[0, src], wg[1, src]], axis=1)
        acc = acc + dot(lhs, rhs)
    wait_home(bg, r_b)
    wait_home(sg, r_sg)
    bias = jnp.concatenate([bg[0, 0], bg[1, 0]], axis=1)[0:1]
    u0 = acc + bias
    t0 = jnp.tanh(GELU_C * (u0 + 0.044715 * (u0 * u0 * u0)))
    hid[...] = (u0 * (0.5 * (1.0 + t0))).astype(BF16)
    second = sg[...].reshape(256, 512)
    part[...] = dot(hid[...], second).reshape(2, 128, 512)
    c_p = send(part.at[1 - k], part_in, sib)
    gd[...] = 0.5 * (1.0 + t0) + 0.5 * u0 * (1.0 - t0 * t0) * (GELU_C * (1.0 + 3.0 * 0.044715 * (u0 * u0)))
    c_p.wait_recv()
    summed = (part[k] + part_in[...]).reshape(4, 32, 512)
    zown[...] = summed
    zs[...] = summed.astype(BF16)
    c_f = {}
    for e in (1, 3, 2):
        c_f[e] = send(zs.at[plus(zl, e)], zr.at[e - 1], dev(zz=plus(zl, e)))
    for zz in range(4):
        for xx in range(4):
            gt[zz * 2 + xx // 2, pl.ds((xx % 2) * 128, 128)] = g[zz, xx].reshape(256, 128).T
    total = zown[zl]
    for e in (1, 3, 2):
        c_f[e].wait_recv()
        total = total + zr[e - 1].astype(F32)
    squashed = jnp.tanh(total)
    sq[...] = squashed
    f[x, k, zl] = squashed.astype(BF16)

    own_piece = f.at[x, k, zl]
    c_fz = {e: send(own_piece, own_piece, dev(zz=plus(zl, e))) for e in (1, 3, 2)}
    c_fx = {}
    c_fp = {}
    for e in ORDER:
        if e:
            c_fz[e].wait_recv()
        piece = f.at[x, k, minus(zl, e)]
        c_fp[e] = send(piece, piece, sib)
        for d in (1, 3, 2):
            c_fx[d, e] = send(piece, piece, dev(xx=plus(x, d)))
    c_fs = {}

    def forward(d):
        for e in ORDER:
            c_fx[d, e].wait_recv()
        block = f.at[minus(x, d), k]
        c_fs[d] = send(block, block, sib)

    c_pair = {}
    c_xr = {}

    def finish_pair(i):
        c_pair[i].wait_recv()
        both = rp[i, k].astype(F32) + prv[i].astype(F32)
        if i == 0:
            xown[...] = both
        else:
            xs_out[i - 1] = both.astype(BF16)
            c_xr[i] = send(xs_out.at[i - 1], xr.at[i - 1], dev(xx=minus(x, ORDER[i])))

    def weigh(i, first, last):
        xx = minus(x, ORDER[i])
        here = slice(256 * i, 256 * i + 256)
        wide = f[xx].reshape(256, 512).astype(F32)
        fn = jnp.sum(wide * wide, axis=1, keepdims=True) * scale

        def tile(t, carry):
            inner = dot(f[xx].reshape(256, 512), ct[t])
            low = jnp.exp2((2.0 * scale) * inner - (fn + cn[t, 0:1])).astype(BF16)
            weighted = kg[xx, t] * low.astype(F32)
            kb[t, here] = low
            wb[t, here] = weighted.astype(BF16)
            rs[i] += (weighted[:, 0:128] + weighted[:, 128:256]) + (weighted[:, 256:384] + weighted[:, 384:512])
            cs[t] += jnp.sum(weighted.reshape(32, 8, 512), axis=0)
            return carry

        lax.fori_loop(first, last, tile, 0)

    c_cg = {}

    def center_out(t):
        column = jnp.sum(cs[t], axis=0, keepdims=True)
        grad = -factor * (column * ct[t].astype(F32) - dot(ft[...], wb[t]))
        cgs[:, t] = grad.astype(BF16).reshape(4, 128, 512)
        for e in (1, 3, 2):
            c_cg[t, e] = send(cgs.at[plus(y, e), t], cgr.at[e - 1, t], dev(yy=plus(y, e)))

    def wait_slots(ref, first, own):
        for j in range(4):
            @pl.when(own != j)
            def _():
                pltpu.make_async_copy(ref.at[j], ref.at[j], rsem.at[first + j]).wait()

    c_ch = {}

    def center_sum(t):
        s = cgs[y, t].astype(F32)
        for e in (1, 3, 2):
            c_cg[t, e].wait_recv()
            s = s + cgr[e - 1, t].astype(F32)
        s = s.reshape(2, 64, 512)
        cgh[t] = s.astype(BF16)
        o_cg[:, t * 512:t * 512 + 512] = jnp.where(h == 0, s[0], s[1])
        c_ch[t] = send(cgh.at[t, 1 - h], cghr.at[t], dev(hh=1 - h))

    def head_sums(i):
        xx = minus(x, ORDER[i])
        here = slice(256 * i, 256 * i + 256)
        low = jnp.concatenate([kb[t, here] for t in range(4)], axis=1)
        rp[i, :, :, 512:] = dot(low, qp[...]).astype(BF16).reshape(2, 128, 128)
        low = jnp.concatenate([wb[t, here] for t in range(4)], axis=1)
        rows = jnp.sum(rs[i], axis=1, keepdims=True)
        fgrad = -factor * (rows * f[xx].reshape(256, 512).astype(F32) - dot(low, ctr[...]))
        rp[i, :, :, :512] = fgrad.astype(BF16).reshape(2, 128, 512)
        c_pair[i] = send(rp.at[i, 1 - k], prv.at[i], sib)

    for e in ORDER:
        c_fp[e].wait_recv()
    for i, d in enumerate(ORDER):
        if i:
            c_fs[d].wait_recv()
        ft[:, 256 * i:256 * i + 256] = f[minus(x, d)].reshape(256, 512).T
        if i < 3:
            weigh(i, 0, 2)
        if i == 0:
            forward(1)
            forward(3)
        if i == 1:
            forward(2)
    weigh(3, 0, 1)
    center_out(0)
    weigh(3, 1, 2)
    center_out(1)
    for i in (1, 2, 3, 0):
        weigh(i, 2, 4)
        if i != 1:
            finish_pair((i + 3) % 4)
        head_sums(i)
    r_cf = new("r", 4)
    turned = jnp.concatenate([cott[minus(x, d)] for d in ORDER], axis=1)[0:112]
    for t in range(4):
        cfs[t] = dot(turned, kb[t]).astype(BF16)
    for e in (1, 3, 2):
        send(cfs.at[plus(y, e)], cfr.at[y], dev(yy=plus(y, e)), r_cf + y)
    cfr[y] = cfs[y]
    finish_pair(0)

    total = xown[...]
    for i in (1, 2, 3):
        c_xr[i].wait_recv()
        total = total + xr[i - 1].astype(F32)
    total = total.reshape(4, 32, 640)
    z2own[...] = total
    z2[...] = total.astype(BF16)
    c_z2 = {e: send(z2.at[plus(zl, e)], z2r.at[e - 1], dev(zz=plus(zl, e))) for e in (1, 3, 2)}
    center_out(2)
    center_out(3)
    center_sum(0)
    center_sum(1)
    total = z2own[zl]
    for e in (1, 3, 2):
        c_z2[e].wait_recv()
        total = total + z2r[e - 1].astype(F32)
    o_pred[...] = total[:, 512:612]
    phi = (total[:, :512] * (1.0 - sq[...] * sq[...])).astype(BF16)
    ph[k, zl] = phi
    c_ph = {e: send(ph.at[k, zl], ph.at[k, zl], dev(zz=plus(zl, e))) for e in (1, 3, 2)}
    c_phs = []
    for e in ORDER:
        if e:
            c_ph[e].wait_recv()
        piece = ph.at[k, minus(zl, e)]
        c_phs.append(send(piece, piece, sib))
    for cp in c_phs:
        cp.wait_recv()

    phi_all = ph[...].reshape(256, 512)
    hgrad = lax.dot_general(phi_all, sg[...].reshape(256, 512), (((1,), (1,)), ((), ())), preferred_element_type=F32)
    pgrad = hgrad * gd[...]
    bias_grad = jnp.sum(pgrad, axis=0, keepdims=True)
    plow = pgrad.astype(BF16)
    phit = phi_all.T
    bias_rows = jnp.broadcast_to(bias_grad, (16, 256)).astype(BF16)
    second_grad = dot(phit, hid[...]).astype(BF16)
    for yy in range(4):
        for hh in range(2):
            q = 2 * yy + hh
            grad = dot(gt[q], plow).astype(BF16)
            tt[yy, hh] = grad[0:192]
            rest = jnp.concatenate([grad[192:256], second_grad[64 * q:64 * q + 64], bias_rows], axis=0)
            tb[0, hh, yy] = rest[:, :128]
            tb[1, hh, yy] = rest[:, 128:]

    def to_units(source, target, first):
        for j in range(2):
            for hh in range(2):
                sid = new("s")
                mine = jnp.logical_and(x == 2 * k + j, k == hh)
                src, dst, rid = source.at[j, hh], target.at[x], first + x
                x_sends.append((src, sid, mine))

                @pl.when(mine)
                def _():
                    pltpu.make_async_copy(src, dst, rsem.at[rid]).start()

                @pl.when(jnp.logical_not(mine))
                def _():
                    remote(src, dst, dev(xx=2 * k + j, kk=hh), sid, rid).start()

    def wait_units(ref, first):
        for j in range(4):
            pltpu.make_async_copy(ref.at[j], ref.at[j], rsem.at[first + j]).wait()

    x_sends = []
    r_vb = new("r", 4)
    to_units(tb, vb, r_vb)
    r_t = new("r", 4)
    for e in (2, 1, 3):
        send(tt.at[plus(y, e)], tr.at[y], dev(yy=plus(y, e)), r_t + y)
    tr[y] = tt[y]
    wait_slots(cfr, r_cf, y)
    s = (cfr[0].astype(F32) + cfr[1].astype(F32)) + (cfr[2].astype(F32) + cfr[3].astype(F32))
    cfh[...] = s.astype(BF16)
    c_cfh = send(cfh, cfhr, dev(hh=1 - h))
    wait_units(vb, r_vb)
    s = (vb[0].astype(F32) + vb[1].astype(F32)) + (vb[2].astype(F32) + vb[3].astype(F32))
    ub[...] = s.astype(BF16)
    r_w2 = new("r", 4)
    for e in (2, 1, 3):
        send(ub.at[plus(y, e)], yb.at[y], dev(yy=plus(y, e)), r_w2 + y)
    yb[y] = ub[y]

    center_sum(2)
    center_sum(3)

    wait_slots(tr, r_t, y)
    for hh in range(2):
        s = (tr[0, hh].astype(F32) + tr[1, hh].astype(F32)) + (tr[2, hh].astype(F32) + tr[3, hh].astype(F32))
        low = s.astype(BF16)
        u[0, hh] = low[:, :128]
        u[1, hh] = low[:, 128:]
    r_v = new("r", 4)
    to_units(u, v, r_v)

    c_cfh.wait_recv()
    cfo[y] = (cfh[...].astype(F32) + cfhr[...].astype(F32)).astype(BF16)
    r_o = new("r", 4)
    for e in (1, 3, 2):
        send(cfo.at[y], cfo.at[y], dev(yy=plus(y, e)), r_o + y)

    wait_slots(yb, r_w2, y)
    s = (yb[0].astype(F32) + yb[1].astype(F32)) + (yb[2].astype(F32) + yb[3].astype(F32))
    mix[192:336] = s
    mix[336:384] = jnp.zeros((48, 128), F32)
    wait_units(v, r_v)
    mix[0:192] = (v[0].astype(F32) + v[1].astype(F32)) + (v[2].astype(F32) + v[3].astype(F32))
    hs[...] = mix[...].T.astype(BF16).reshape(2, 64, 384)
    s_across, s_also, r_across, s_last, r_last = new("s"), new("s"), new("r"), new("s"), new("r")

    @pl.when(k != h)
    def _():
        remote(hs.at[k], hb, dev(hh=1 - h, kk=k), s_across, r_across).start()
        remote(hs.at[1 - k], hb, dev(hh=1 - h, kk=1 - k), s_also, r_across).start()

    @pl.when(k == h)
    def _():
        remote(hs.at[1 - k], ha, sib, s_last, r_last).start()

    for t in range(4):
        c_ch[t].wait_recv()
        o_cg[:, t * 512:t * 512 + 512] += cghr[t].astype(F32)

    wait_slots(cfo, r_o, y)
    for t in range(4):
        o_coef[:, t * 512:t * 512 + 512] = cfo[t, 0:100].astype(F32)

    @pl.when(k == h)
    def _():
        ha[...] = hs[k]

    @pl.when(k != h)
    def _():
        pltpu.make_async_copy(ha, ha, rsem.at[r_last]).wait()

    pltpu.make_async_copy(hb, hb, rsem.at[r_across]).wait()
    tot = ha[...].astype(F32) + hb[...].astype(F32)
    o_first[...] = tot[:, 0:256]
    o_second[...] = tot[:, 256:320]
    o_bias[...] = tot[:, 256:384].T[64:65]

    for cp in sent:
        cp.wait_send()
    for src, dst, sid in homes:
        @pl.when(k != x // 2)
        def _():
            pltpu.make_async_copy(src, src, ssem.at[sid]).wait()
    for src, sid, mine in x_sends:
        @pl.when(jnp.logical_not(mine))
        def _():
            pltpu.make_async_copy(src, src, ssem.at[sid]).wait()

    @pl.when(k != h)
    def _():
        pltpu.make_async_copy(ha, ha, ssem.at[s_across]).wait()
        pltpu.make_async_copy(ha, ha, ssem.at[s_also]).wait()

    @pl.when(k == h)
    def _():
        pltpu.make_async_copy(ha, ha, ssem.at[s_last]).wait()


SCRATCH = (
    ("embt", (64, 1024), BF16), ("w1t", (64, 1024), BF16), ("ctr", (2048, 512), BF16), ("coeft", (100, 2048), BF16), ("cott_in", (100, 1024), BF16),
    ("emb_sib", (64, 1024), BF16), ("emb_all", (4, 4, 2, 32, 128), BF16), ("w_sib", (64, 1024), BF16),
    ("w_pair", (2, 512, 128), BF16), ("b_mine", (8, 128), F32), ("b_sib", (8, 128), F32), ("b_pair", (8, 128), F32),
    ("wg", (2, 4, 512, 128), BF16), ("sg", (2, 2, 64, 512), BF16), ("bg", (2, 2, 8, 128), F32),
    ("g", (4, 4, 2, 4, 32, 128), BF16), ("gt", (8, 256, 256), BF16),
    ("hid", (256, 256), BF16), ("gd", (256, 256), F32),
    ("part", (2, 128, 512), F32), ("part_in", (128, 512), F32),
    ("zs", (4, 32, 512), BF16), ("zown", (4, 32, 512), F32), ("zr", (3, 32, 512), BF16), ("sq", (32, 512), F32),
    ("f", (4, 2, 4, 32, 512), BF16), ("ft", (512, 1024), BF16), ("ct", (4, 512, 512), BF16),
    ("qp", (2048, 128), BF16), ("qt", (4, 128, 512), BF16), ("cn", (4, 8, 512), F32),
    ("cot_pad", (128, 1024), BF16), ("cot_all", (4, 4, 2, 32, 128), BF16), ("cotp", (4, 256, 128), BF16), ("cott", (4, 128, 256), BF16),
    ("kg", (4, 4, 256, 512), F32), ("kb", (4, 1024, 512), BF16), ("wb", (4, 1024, 512), BF16),
    ("rs", (4, 256, 128), F32), ("cs", (4, 8, 512), F32),
    ("rp", (4, 2, 128, 640), BF16), ("prv", (4, 128, 640), BF16), ("xown", (128, 640), F32),
    ("xs_out", (3, 128, 640), BF16), ("xr", (3, 128, 640), BF16),
    ("z2", (4, 32, 640), BF16), ("z2own", (4, 32, 640), F32), ("z2r", (3, 32, 640), BF16), ("ph", (2, 4, 32, 512), BF16),
    ("cgs", (4, 4, 128, 512), BF16), ("cgr", (3, 4, 128, 512), BF16), ("cgh", (4, 2, 64, 512), BF16), ("cghr", (4, 64, 512), BF16),
    ("cfs", (4, 112, 512), BF16), ("cfr", (4, 112, 512), BF16), ("cfh", (112, 512), BF16), ("cfo", (4, 112, 512), BF16), ("cfhr", (112, 512), BF16),
    ("tt", (4, 2, 192, 256), BF16), ("tr", (4, 2, 192, 256), BF16), ("u", (2, 2, 192, 128), BF16), ("v", (4, 192, 128), BF16),
    ("tb", (2, 2, 4, 144, 128), BF16), ("vb", (4, 4, 144, 128), BF16), ("ub", (4, 144, 128), BF16), ("yb", (4, 144, 128), BF16),
    ("mix", (384, 128), F32), ("hs", (2, 64, 384), BF16), ("ha", (64, 384), BF16), ("hb", (64, 384), BF16),
)


def finish(*refs):
    n = len(refs) // 2
    for i in range(n):
        refs[n + i][...] = refs[i][...]


def body(embeddings, first_weight, first_bias, second_weight, centers, coefficients, cotangent):
    args = (
        embeddings.T,
        first_weight.T,
        first_bias.reshape(1, 64),
        second_weight,
        centers,
        coefficients.T,
        cotangent.T,
    )
    vmem = pl.BlockSpec(memory_space=pltpu.VMEM)
    anywhere = pl.BlockSpec(memory_space=pl.ANY)
    outs = (
        jax.ShapeDtypeStruct((32, 100), F32),
        jax.ShapeDtypeStruct((64, 256), F32),
        jax.ShapeDtypeStruct((64, 64), F32),
        jax.ShapeDtypeStruct((1, 64), F32),
        jax.ShapeDtypeStruct((64, 2048), F32),
        jax.ShapeDtypeStruct((100, 2048), F32),
    )
    made = pl.pallas_call(
        kernel,
        out_shape=outs,
        in_specs=[anywhere, anywhere, vmem, anywhere, anywhere, anywhere, anywhere],
        out_specs=[vmem] * len(outs),
        scratch_shapes=[pltpu.VMEM(shape, dtype) for name, shape, dtype in SCRATCH]
        + [pltpu.SemaphoreType.DMA((SEMS,)), pltpu.SemaphoreType.DMA((SEMS,))],
        compiler_params=pltpu.CompilerParams(collective_id=0, has_side_effects=True, vmem_limit_bytes=60 << 20),
        name="layer",
    )(*args)
    predictions, grad_first, grad_second, grad_bias, grad_centers, grad_coefs = pl.pallas_call(
        finish,
        out_shape=outs,
        in_specs=[vmem] * len(outs),
        out_specs=[vmem] * len(outs),
        name="finish",
    )(*made)
    return (predictions, grad_first.T, grad_bias[0], grad_second, grad_centers.T, grad_coefs.T)


def solution(mesh):
    placed = (
        P("dp", "center"),
        P(None, "center"),
        P("center"),
        P("center", None),
        P("center", None),
        P("center", None),
        P("dp", None),
    )
    return jax.shard_map(
        body,
        mesh=mesh,
        in_specs=placed,
        out_specs=(
            P(("dp", "center"), None),
            P("dp", "center"),
            P("center"),
            P("center", "dp"),
            P("center", "dp"),
            P("center", None),
        ),
        check_vma=False,
    )
```
